32 devices in a mesh: groups: 2 (over x), facet: 16 (over z, y, core).
Axes of the slice: x: 2, y: 2, z: 4, core: 2. Of those that a mesh axis runs over, the one named last changes fastest.
Arguments:
- visibility: bfloat16 [16384, 128], P(('groups', 'facet')), parts along dimension 0, may hold values from -6 to 6
- facet_of: int32 [16384, 1], P(('groups', 'facet')), parts along dimension 0, may hold values from 0 to 15; in each aligned block of 512 rows (0 to 511, 512 to 1023, ...) at most 64 rows name the same one
- cell_of: int32 [16384], P(('groups', 'facet')), parts along dimension 0, may hold values from 0 to 16383
- taper: bfloat16 [32768, 128], P(('groups', 'facet')), parts along dimension 0, may hold values from -1 to 1
- model: bfloat16 [524288, 128], P(('groups', 'facet')), parts along dimension 0, may hold values from -6 to 6
Outputs:
- model_next: bfloat16 [524288, 128], P(('groups', 'facet')), parts along dimension 0
- residual: bfloat16 [16384, 128], P(('groups', 'facet')), parts along dimension 0
The draws below stay inside these ranges and needn't reach their ends.
There are 2 independent parts, one for each index of `groups`. The reference program is written for one: setup_inputs(seed, part) draws one part's arguments, and reference() takes and returns one part's arrays. A program takes and returns all parts, laid end to end along the dimension named above; each array names one. Nothing has to cross between parts.
Inputs may be any that keep to these rules, and one draw needn't show every extreme that they name: `facet_of`: every facet is named by some row; at most 64 rows of one device name one facet, and in every draw some device has exactly 64 rows for one facet.
All inputs are finite; a program needn't handle non-finite values.
Results may differ from the reference program's by a relative error of at most 0.0058.
Values may be sent and summed in bfloat16 or wider, within the bound.
A program may use at most 128 MiB of HBM per device.

```python
import math
import jax
import jax.numpy as jnp
import numpy as np
from jax import lax

CHAN = 64
GU = 128
GV = 128
R_DEV = 512
CELLS = 16384
FACETS = 16
ROWS = 8192
CAP = 64


def place_ends(array, own_key, smallest, largest):
    longest = array.shape.index(max(array.shape))
    spots = []
    for shift in (0, 1):
        where = [jax.random.randint(jax.random.fold_in(own_key, axis), (), 0, length) for axis, length in enumerate(array.shape)]
        where[longest] = (where[longest] + shift) % array.shape[longest]
        spots.append(tuple(where))
    return array.at[spots[0]].set(smallest).at[spots[1]].set(largest)


def block_levels(own_key, shape, shards, smallest, top_value):
    factor_of, own = 1.0, jax.random.fold_in(own_key, 6)
    for axis_at, shards_of in shards:
        draws = jnp.exp(jax.random.uniform(jax.random.fold_in(own, axis_at), (shards_of,), jnp.float32, smallest / len(shards), top_value / len(shards)))
        factor_of = factor_of * jnp.repeat(draws, shape[axis_at] // shards_of).reshape([-1 if axis == axis_at else 1 for axis in range(len(shape))])
    return factor_of


def shared_out(key, own, number, rows, amount, top, limit, lean):
    ranking = jax.random.permutation(key, amount)
    crowded, common = portions_of(amount, rows * top, limit, lean, True), portions_of(amount, rows * top, limit, lean, False)
    places = jnp.arange(amount)

    def named(lengths, offset_by):
        used = int((lengths > 0).sum())
        fixed = max(1, used // 4)
        shifted = fixed + (places - fixed + offset_by * (used - fixed)) % max(1, amount - fixed)
        return jnp.zeros((amount,), jnp.int32).at[ranking[jnp.where(places < fixed, places, shifted)]].set(jnp.asarray(lengths, jnp.int32))

    lengths = jnp.where(number % 4 == 0, named(crowded, number // 4), named(common, number - number // 4 - 1))
    mixed = jax.random.permutation(jax.random.fold_in(own, 3), amount)
    donor, receiver = mixed[0:amount // 2 * 2:2], mixed[1:amount // 2 * 2:2]
    margin = jnp.minimum(lengths[donor] - 1, limit - lengths[receiver]) // 2
    margin = jnp.where((donor == ranking[0]) | (receiver == ranking[0]) | (lengths[receiver] == 0), 0, jnp.maximum(margin, 0))
    shifted = jax.random.randint(jax.random.fold_in(own, 4), (amount // 2,), 0, 1 << 20) % (margin + 1)
    lengths = lengths.at[donor].add(-shifted).at[receiver].add(shifted)
    items = jnp.searchsorted(jnp.cumsum(lengths), jnp.arange(rows * top), side="right").astype(jnp.int32)
    grid = items.reshape(top, rows).T
    grid = grid[jax.random.permutation(jax.random.fold_in(own, 1), rows)]
    offset_by = jax.random.randint(jax.random.fold_in(own, 2), (rows, 1), 0, top)
    return jnp.take_along_axis(grid, (jnp.arange(top)[None, :] + offset_by) % top, axis=1)


def portions_of(count, total, limit, skew, full):
    weights = [(1 << 20) // math.isqrt(standing ** skew) + 1 for standing in range(1, count + 1)]
    largest = limit if full else min(limit, max(-(-total // count), total * weights[0] // sum(weights)))
    least = 1 if total - largest >= count - 1 else 0
    counts, spare = [largest] + [least] * (count - 1), total - largest - least * (count - 1)
    while spare > 0:
        movable = [i for i in range(1, count) if counts[i] < largest] or [i for i in range(1, count) if counts[i] < limit]
        pool, remaining = sum([weights[i] for i in movable]), spare
        for i in movable:
            addition = min(limit - counts[i], max(1, remaining * weights[i] // pool), spare)
            counts[i] = counts[i] + addition
            spare = spare - addition
    return np.array(counts)


def bell_draw(stream_key, dims, width, limit, split=(), held_as=jnp.bfloat16):
    level = block_levels(stream_key, dims, split, -0.22, 0.18) if split else 1.0
    drawn = jax.random.normal(stream_key, dims, jnp.float32) * width * level
    return jnp.minimum(jnp.maximum(drawn, -limit), limit).astype(held_as)


def setup_inputs(seed: int = 0, part: int = 0) -> dict:
    streams_of = jax.random.split(jax.random.key(seed), 6)
    part_splits = jax.random.split(jax.random.fold_in(streams_of[5], part), 6)
    visibility = bell_draw(part_splits[0], (ROWS, 2 * CHAN), 1.0, 6.0, ((0, 16),))
    facet_of_keys = jax.random.split(jax.random.fold_in(part_splits[1], 1), ROWS // R_DEV)
    facet_of_turns = jax.random.permutation(jax.random.fold_in(part_splits[1], 3), ROWS // R_DEV)
    facet_of = jax.vmap(lambda own, number: shared_out(jax.random.fold_in(part_splits[1], 2), own, number, R_DEV, FACETS, 1, CAP, 2))(facet_of_keys, facet_of_turns).reshape((ROWS, 1))
    cell_of = place_ends(jax.random.randint(part_splits[2], (ROWS,), 0, CELLS), jax.random.fold_in(part_splits[2], 1), 0, CELLS - 1).astype(jnp.int32)
    taper = jnp.clip(jax.random.uniform(part_splits[3], (CELLS, 2 * CHAN), jnp.float32, -1.0, 1.0) * block_levels(part_splits[3], (CELLS, 2 * CHAN), ((0, 16),), -0.4, 0.0), -1.0, 1.0).astype(jnp.bfloat16)
    model = bell_draw(part_splits[4], (FACETS * CELLS, 2 * CHAN), 1.0, 6.0, ((0, 16),))
    return dict(visibility=visibility, facet_of=facet_of, cell_of=cell_of, taper=taper, model=model)


loop_gain = 0.1

def complex_product(left, right):
    midway = left.shape[-1] // 2
    left_real, left_imaginary = (left[..., :midway], left[..., midway:])
    right_real, right_imaginary = (right[..., :midway], right[..., midway:])
    return jnp.concatenate([left_real * right_real - left_imaginary * right_imaginary, left_real * right_imaginary + left_imaginary * right_real], -1)

def conjugate(values):
    midway = values.shape[-1] // 2
    return jnp.concatenate([values[..., :midway], -values[..., midway:]], -1)

def dft_table(length, orient):
    ordinal = jnp.arange(length, dtype=jnp.int32)
    phases = ordinal[:, None] * ordinal[None, :] % length
    angles = phases.astype(jnp.float32) * (2.0 * math.pi / length)
    return jnp.concatenate([jnp.cos(angles), orient * jnp.sin(angles)], 0).astype(jnp.bfloat16)

def along_axis(volume, length, orient, pattern, axis):
    table = dft_table(length, orient).astype(jnp.float32)
    stacked = jnp.einsum(pattern, table, volume.astype(jnp.float32), precision=lax.Precision.HIGHEST)
    leading = lax.slice_in_dim(stacked, 0, length, axis=axis)
    second = lax.slice_in_dim(stacked, length, 2 * length, axis=axis)
    midway = volume.shape[-1] // 2
    joined = jnp.concatenate([leading[..., :midway] - second[..., midway:], leading[..., midway:] + second[..., :midway]], -1)
    return joined.astype(jnp.bfloat16)

def transform(plane, orient, extent_u, extent_v):
    columns = plane.shape[-1]
    volume = plane.reshape(extent_u, extent_v, columns)
    volume = along_axis(volume, extent_u, orient, 'pu,uvc->pvc', 0)
    volume = along_axis(volume, extent_v, orient, 'qv,pvc->pqc', 1)
    return volume.reshape(extent_u * extent_v, columns)

def reference(visibility, facet_of, cell_of, taper, model):
    target = facet_of[:, 0]
    vis_wide = visibility.astype(jnp.float32)
    panel = taper.astype(jnp.float32)
    conj_panel = conjugate(panel)
    model_wide = model.astype(jnp.float32).reshape(FACETS, CELLS, 2 * CHAN)

    def per_facet(predicted, inputs):
        facet_number, model_block = inputs
        member = target == facet_number
        segment = jnp.where(member, cell_of, CELLS).astype(jnp.int32)
        grid_sum = jax.ops.segment_sum(vis_wide, segment, num_segments=CELLS + 1)[:CELLS]
        row_count = jnp.sum(member.astype(jnp.float32))
        tapered = complex_product(grid_sum, panel).astype(jnp.bfloat16)
        dirty_image = transform(tapered, -1, GU, GV).astype(jnp.float32) / jnp.sqrt(row_count)
        model_sum = model_block + loop_gain * dirty_image
        model_next = model_sum.astype(jnp.bfloat16)
        spectrum = transform(model_next, 1, GU, GV).astype(jnp.float32) / math.sqrt(CELLS)
        model_grid = complex_product(spectrum, conj_panel)
        picked = jnp.take(model_grid, cell_of.astype(jnp.int32), axis=0)
        predicted = predicted + jnp.where(member[:, None], picked, jnp.zeros_like(picked))
        return (predicted, model_next)
    predicted, stacked = lax.scan(per_facet, jnp.zeros_like(vis_wide), (jnp.arange(FACETS, dtype=jnp.int32), model_wide))
    return (stacked.reshape(FACETS * CELLS, 2 * CHAN), (vis_wide - predicted).astype(jnp.bfloat16))
```

```python
import functools
import math

import jax
import jax.numpy as jnp
from jax import lax
from jax.experimental import pallas as pl
from jax.experimental.pallas import tpu as pltpu
from jax.sharding import PartitionSpec as P

LOOP_GAIN = 0.1


def dft_table(length, orient):
    ordinal = jnp.arange(length, dtype=jnp.int32)
    phases = ordinal[:, None] * ordinal[None, :] % length
    angles = phases.astype(jnp.float32) * (2.0 * math.pi / length)
    return jnp.concatenate([jnp.cos(angles), orient * jnp.sin(angles)], 1).astype(jnp.bfloat16)


def turned(values):
    half = values.shape[-1] // 2
    lane = lax.broadcasted_iota(jnp.int32, values.shape, 1)
    rolled = pltpu.roll(values, half, 1)
    return jnp.where(lane < half, -rolled, rolled)


def stage(table, first, second):
    top = jnp.concatenate([first, second], 1).astype(jnp.bfloat16)
    low = jnp.concatenate([turned(first), turned(second)], 1).astype(jnp.bfloat16)
    return jnp.dot(table, jnp.concatenate([top, low], 0), preferred_element_type=jnp.float32)


def cycle_kernel(gu, gv, grid_at, panel_at, scale, rows, panel, model, minus, plus,
                 model_next, answer, wide, cross, picked):
    cells = gu * gv
    slots, columns = rows.shape
    half = columns // 2

    chunk = 512

    @pl.loop(0, cells // chunk)
    def _(i):
        at = pl.ds(pl.multiple_of(i * chunk, chunk), chunk)
        wide[at, :] = jnp.zeros((chunk, columns), jnp.float32)
        cross[at, :] = panel[at, :].astype(jnp.float32)

    wide[pl.ds(cells, 8), :] = jnp.zeros((8, columns), jnp.float32)

    @pl.loop(0, slots // 16)
    def _(i):
        base = pl.multiple_of(i * 16, 16)
        for k in range(16):
            picked[pl.ds(base + k, 1), :] = cross[pl.ds(panel_at[base + k], 1), :]

    lane = lax.broadcasted_iota(jnp.int32, (slots, columns), 1)
    kernel_rows = picked[...]
    swapped = pltpu.roll(kernel_rows, half, 1)
    real = jnp.where(lane < half, kernel_rows, swapped)
    imag = jnp.where(lane < half, swapped, kernel_rows)
    values = rows[...].astype(jnp.float32)
    cross[pl.ds(0, slots), :] = values * real + turned(values) * imag

    @pl.loop(0, slots // 16)
    def _(i):
        base = pl.multiple_of(i * 16, 16)
        for k in range(16):
            at = pl.ds(grid_at[base + k], 1)
            wide[at, :] += cross[pl.ds(base + k, 1), :]

    @pl.loop(0, gv // 2)
    def _(i):
        base = pl.multiple_of(i * (2 * gu), 2 * gu)
        out = stage(minus[...], wide[pl.ds(base, gu), :], wide[pl.ds(base + gu, gu), :])
        cross[pl.ds(2 * i, gu, stride=gv), :] = out[:, :columns]
        cross[pl.ds(2 * i + 1, gu, stride=gv), :] = out[:, columns:]

    gain = scale[0]

    @pl.loop(0, gu // 2)
    def _(i):
        base = pl.multiple_of(i * (2 * gv), 2 * gv)
        low, high = pl.ds(base, gv), pl.ds(base + gv, gv)
        out = stage(minus[...], cross[low, :], cross[high, :])
        first = (model[low, :].astype(jnp.float32) + gain * out[:, :columns]).astype(jnp.bfloat16)
        second = (model[high, :].astype(jnp.float32) + gain * out[:, columns:]).astype(jnp.bfloat16)
        model_next[low, :] = first
        model_next[high, :] = second
        out = stage(plus[...], first.astype(jnp.float32), second.astype(jnp.float32))
        wide[pl.ds(2 * i, gv, stride=gu), :] = out[:, :columns]
        wide[pl.ds(2 * i + 1, gv, stride=gu), :] = out[:, columns:]

    @pl.loop(0, gv // 2)
    def _(i):
        base = pl.multiple_of(i * (2 * gu), 2 * gu)
        out = stage(plus[...], wide[pl.ds(base, gu), :], wide[pl.ds(base + gu, gu), :])
        cross[pl.ds(base, gu), :] = out[:, :columns]
        cross[pl.ds(base + gu, gu), :] = out[:, columns:]

    cross[pl.ds(cells, 8), :] = jnp.zeros((8, columns), jnp.float32)

    @pl.loop(0, slots // 16)
    def _(i):
        base = pl.multiple_of(i * 16, 16)
        for k in range(16):
            wide[pl.ds(base + k, 1), :] = cross[pl.ds(grid_at[base + k], 1), :]

    kernel_rows = picked[...]
    swapped = pltpu.roll(kernel_rows, half, 1)
    real = jnp.where(lane < half, kernel_rows, swapped)
    imag = jnp.where(lane < half, swapped, kernel_rows)
    found = wide[pl.ds(0, slots), :] * (1.0 / math.sqrt(cells))
    predicted = found * real - turned(found) * imag
    answer[...] = (rows[...].astype(jnp.float32) - predicted).astype(jnp.bfloat16)


def run_cycle(gu, gv, grid_at, panel_at, scale, rows, panel, model):
    cells = gu * gv
    slots, columns = rows.shape
    smem = pl.BlockSpec(memory_space=pltpu.SMEM)
    vmem = pl.BlockSpec(memory_space=pltpu.VMEM)
    return pl.pallas_call(
        functools.partial(cycle_kernel, gu, gv),
        out_shape=(
            jax.ShapeDtypeStruct((cells, columns), jnp.bfloat16),
            jax.ShapeDtypeStruct((slots, columns), jnp.bfloat16),
        ),
        in_specs=[smem] * 3 + [vmem] * 5,
        out_specs=(vmem, vmem),
        scratch_shapes=[
            pltpu.VMEM((cells + 8, columns), jnp.float32),
            pltpu.VMEM((cells + 8, columns), jnp.float32),
            pltpu.VMEM((slots, columns), jnp.float32),
        ],
        compiler_params=pltpu.CompilerParams(vmem_limit_bytes=50 * 1024 * 1024),
    )(grid_at, panel_at, scale, rows, panel, model, dft_table(gu, -1), dft_table(gu, 1))


def body(visibility, facet_of, cell_of, taper, model):
    peers = lax.axis_size("facet")
    local_rows, columns = visibility.shape
    capacity = 2 * local_rows // peers
    slots = peers * capacity
    cells = model.shape[0]
    gu = gv = math.isqrt(cells)

    panel = lax.all_gather(taper, "facet", axis=0, tiled=True)

    target = facet_of[:, 0]
    order = jnp.arange(local_rows, dtype=jnp.int32)
    earlier = (order[:, None] > order[None, :]) & (target[:, None] == target[None, :])
    position = target * capacity + jnp.sum(earlier.astype(jnp.int32), axis=1)
    placed = jnp.arange(slots, dtype=jnp.int32)[:, None] == position[None, :]
    send_rows = jnp.dot(
        placed.astype(jnp.bfloat16), visibility, preferred_element_type=jnp.float32
    ).astype(jnp.bfloat16)
    send_cells = jnp.min(jnp.where(placed, cell_of[None, :], cells), axis=1)

    cell_ids = lax.all_to_all(
        send_cells.reshape(peers, capacity), "facet", split_axis=0, concat_axis=0, tiled=True
    ).reshape(slots)
    rows = lax.all_to_all(
        send_rows.reshape(peers, capacity, columns), "facet", split_axis=0, concat_axis=0, tiled=True
    ).reshape(slots, columns)

    used = cell_ids < cells
    scale = LOOP_GAIN / jnp.sqrt(jnp.sum(used.astype(jnp.float32)))
    grid_at = jnp.where(used, cell_ids % gv * gu + cell_ids // gv, cells)
    panel_at = jnp.minimum(cell_ids, cells - 1)
    model_next, answer = run_cycle(gu, gv, grid_at, panel_at, scale.reshape(1), rows, panel, model)

    returned = lax.all_to_all(
        answer.reshape(peers, capacity, columns), "facet", split_axis=0, concat_axis=0, tiled=True
    ).reshape(slots, columns)
    residual = lax.dot_general(
        placed.astype(jnp.bfloat16), returned, (((0,), (0,)), ((), ())),
        preferred_element_type=jnp.float32,
    ).astype(jnp.bfloat16)
    return (model_next, residual)


def solution(mesh):
    both = ("groups", "facet")
    return jax.shard_map(
        body,
        mesh=mesh,
        in_specs=(P(both, None), P(both, None), P(both), P(both, None), P(both, None)),
        out_specs=(P(both, None), P(both, None)),
        check_vma=False,
    )
```

```python
import functools
import math

import jax
import jax.numpy as jnp
from jax import lax
from jax.experimental import pallas as pl
from jax.experimental.pallas import tpu as pltpu
from jax.sharding import PartitionSpec as P

LOOP_GAIN = 0.1
GROUP = 8
UNROLL = 2


def dft_table(length, orient):
    ordinal = jnp.arange(length, dtype=jnp.int32)
    phases = ordinal[:, None] * ordinal[None, :] % length
    angles = phases.astype(jnp.float32) * (2.0 * math.pi / length)
    return jnp.concatenate([jnp.cos(angles), orient * jnp.sin(angles)], 1).astype(jnp.bfloat16)


def turned(values):
    half = values.shape[-1] // 2
    lane = lax.broadcasted_iota(jnp.int32, values.shape, 1)
    rolled = pltpu.roll(values, half, 1)
    return jnp.where(lane < half, -rolled, rolled)


def stage(table, slabs):
    columns = slabs[0].shape[1]
    top = jnp.concatenate(slabs, 1).astype(jnp.bfloat16)
    low = jnp.concatenate([turned(slab) for slab in slabs], 1).astype(jnp.bfloat16)
    out = jnp.dot(table, jnp.concatenate([top, low], 0), preferred_element_type=jnp.float32)
    return [out[:, k * columns : (k + 1) * columns] for k in range(len(slabs))]


def cycle_kernel(gu, gv, grid_at, panel_at, scale, rows, panel, model, minus, plus,
                 model_next, answer, wide, cross, picked):
    cells = gu * gv
    slots, columns = rows.shape
    half = columns // 2

    chunk = 512

    @pl.loop(0, cells // chunk)
    def _(i):
        at = pl.ds(pl.multiple_of(i * chunk, chunk), chunk)
        wide[at, :] = jnp.zeros((chunk, columns), jnp.float32)
        cross[at, :] = panel[at, :].astype(jnp.float32)

    wide[pl.ds(cells, 8), :] = jnp.zeros((8, columns), jnp.float32)

    @pl.loop(0, slots // 16)
    def _(i):
        base = pl.multiple_of(i * 16, 16)
        for k in range(16):
            picked[pl.ds(base + k, 1), :] = cross[pl.ds(panel_at[base + k], 1), :]

    lane = lax.broadcasted_iota(jnp.int32, (slots, columns), 1)
    kernel_rows = picked[...]
    swapped = pltpu.roll(kernel_rows, half, 1)
    real = jnp.where(lane < half, kernel_rows, swapped)
    imag = jnp.where(lane < half, swapped, kernel_rows)
    values = rows[...].astype(jnp.float32)
    cross[pl.ds(0, slots), :] = values * real + turned(values) * imag

    @pl.loop(0, slots // 16)
    def _(i):
        base = pl.multiple_of(i * 16, 16)
        for k in range(16):
            at = pl.ds(grid_at[base + k], 1)
            wide[at, :] += cross[pl.ds(base + k, 1), :]

    @pl.loop(0, gv // GROUP, unroll=UNROLL)
    def _(i):
        base = pl.multiple_of(i * (GROUP * gu), GROUP * gu)
        out = stage(minus[...], [wide[pl.ds(base + k * gu, gu), :] for k in range(GROUP)])
        for k in range(GROUP):
            cross[pl.ds(GROUP * i + k, gu, stride=gv), :] = out[k]

    gain = scale[0]

    @pl.loop(0, gu // GROUP, unroll=UNROLL)
    def _(i):
        base = pl.multiple_of(i * (GROUP * gv), GROUP * gv)
        at = [pl.ds(base + k * gv, gv) for k in range(GROUP)]
        out = stage(minus[...], [cross[here, :] for here in at])
        updated = []
        for k in range(GROUP):
            value = (model[at[k], :].astype(jnp.float32) + gain * out[k]).astype(jnp.bfloat16)
            model_next[at[k], :] = value
            updated.append(value.astype(jnp.float32))
        out = stage(plus[...], updated)
        for k in range(GROUP):
            wide[pl.ds(GROUP * i + k, gv, stride=gu), :] = out[k]

    @pl.loop(0, gv // GROUP, unroll=UNROLL)
    def _(i):
        base = pl.multiple_of(i * (GROUP * gu), GROUP * gu)
        out = stage(plus[...], [wide[pl.ds(base + k * gu, gu), :] for k in range(GROUP)])
        for k in range(GROUP):
            cross[pl.ds(base + k * gu, gu), :] = out[k]

    cross[pl.ds(cells, 8), :] = jnp.zeros((8, columns), jnp.float32)

    @pl.loop(0, slots // 16)
    def _(i):
        base = pl.multiple_of(i * 16, 16)
        for k in range(16):
            wide[pl.ds(base + k, 1), :] = cross[pl.ds(grid_at[base + k], 1), :]

    kernel_rows = picked[...]
    swapped = pltpu.roll(kernel_rows, half, 1)
    real = jnp.where(lane < half, kernel_rows, swapped)
    imag = jnp.where(lane < half, swapped, kernel_rows)
    found = wide[pl.ds(0, slots), :] * (1.0 / math.sqrt(cells))
    predicted = found * real - turned(found) * imag
    answer[...] = (rows[...].astype(jnp.float32) - predicted).astype(jnp.bfloat16)


def run_cycle(gu, gv, grid_at, panel_at, scale, rows, panel, model):
    cells = gu * gv
    slots, columns = rows.shape
    smem = pl.BlockSpec(memory_space=pltpu.SMEM)
    vmem = pl.BlockSpec(memory_space=pltpu.VMEM)
    return pl.pallas_call(
        functools.partial(cycle_kernel, gu, gv),
        out_shape=(
            jax.ShapeDtypeStruct((cells, columns), jnp.bfloat16),
            jax.ShapeDtypeStruct((slots, columns), jnp.bfloat16),
        ),
        in_specs=[smem] * 3 + [vmem] * 5,
        out_specs=(vmem, vmem),
        scratch_shapes=[
            pltpu.VMEM((cells + 8, columns), jnp.float32),
            pltpu.VMEM((cells + 8, columns), jnp.float32),
            pltpu.VMEM((slots, columns), jnp.float32),
        ],
        compiler_params=pltpu.CompilerParams(vmem_limit_bytes=50 * 1024 * 1024),
    )(grid_at, panel_at, scale, rows, panel, model, dft_table(gu, -1), dft_table(gu, 1))


def body(visibility, facet_of, cell_of, taper, model):
    peers = lax.axis_size("facet")
    local_rows, columns = visibility.shape
    capacity = 2 * local_rows // peers
    slots = peers * capacity
    cells = model.shape[0]
    gu = gv = math.isqrt(cells)

    panel = lax.all_gather(taper, "facet", axis=0, tiled=True)

    target = facet_of[:, 0]
    order = jnp.arange(local_rows, dtype=jnp.int32)
    earlier = (order[:, None] > order[None, :]) & (target[:, None] == target[None, :])
    position = target * capacity + jnp.sum(earlier.astype(jnp.int32), axis=1)
    placed = jnp.arange(slots, dtype=jnp.int32)[:, None] == position[None, :]
    send_rows = jnp.dot(
        placed.astype(jnp.bfloat16), visibility, preferred_element_type=jnp.float32
    ).astype(jnp.bfloat16)
    send_cells = jnp.min(jnp.where(placed, cell_of[None, :], cells), axis=1)

    cell_ids = lax.all_to_all(
        send_cells.reshape(peers, capacity), "facet", split_axis=0, concat_axis=0, tiled=True
    ).reshape(slots)
    rows = lax.all_to_all(
        send_rows.reshape(peers, capacity, columns), "facet", split_axis=0, concat_axis=0, tiled=True
    ).reshape(slots, columns)

    used = cell_ids < cells
    scale = LOOP_GAIN / jnp.sqrt(jnp.sum(used.astype(jnp.float32)))
    grid_at = jnp.where(used, cell_ids % gv * gu + cell_ids // gv, cells)
    panel_at = jnp.minimum(cell_ids, cells - 1)
    model_next, answer = run_cycle(gu, gv, grid_at, panel_at, scale.reshape(1), rows, panel, model)

    returned = lax.all_to_all(
        answer.reshape(peers, capacity, columns), "facet", split_axis=0, concat_axis=0, tiled=True
    ).reshape(slots, columns)
    residual = lax.dot_general(
        placed.astype(jnp.bfloat16), returned, (((0,), (0,)), ((), ())),
        preferred_element_type=jnp.float32,
    ).astype(jnp.bfloat16)
    return (model_next, residual)


def solution(mesh):
    both = ("groups", "facet")
    return jax.shard_map(
        body,
        mesh=mesh,
        in_specs=(P(both, None), P(both, None), P(both), P(both, None), P(both, None)),
        out_specs=(P(both, None), P(both, None)),
        check_vma=False,
    )
```

```python
import functools
import math

import jax
import jax.numpy as jnp
from jax import lax
from jax.experimental import pallas as pl
from jax.experimental.pallas import tpu as pltpu
from jax.sharding import PartitionSpec as P

LOOP_GAIN = 0.1
MESH = pl.DeviceIdType.MESH
GROUP = 8
UNROLL = 2


def dft_table(length, orient):
    ordinal = jnp.arange(length, dtype=jnp.int32)
    phases = ordinal[:, None] * ordinal[None, :] % length
    angles = phases.astype(jnp.float32) * (2.0 * math.pi / length)
    return jnp.concatenate([jnp.cos(angles), orient * jnp.sin(angles)], 1).astype(jnp.bfloat16)


def turned(values):
    half = values.shape[-1] // 2
    lane = lax.broadcasted_iota(jnp.int32, values.shape, 1)
    rolled = pltpu.roll(values, half, 1)
    return jnp.where(lane < half, -rolled, rolled)


def stage(table, slabs):
    columns = slabs[0].shape[1]
    top = jnp.concatenate(slabs, 1).astype(jnp.bfloat16)
    low = jnp.concatenate([turned(slab) for slab in slabs], 1).astype(jnp.bfloat16)
    out = jnp.dot(table, jnp.concatenate([top, low], 0), preferred_element_type=jnp.float32)
    return [out[:, k * columns : (k + 1) * columns] for k in range(len(slabs))]


def cycle_kernel(gu, gv, grid_at, panel_at, scale, rows, panel, model, minus, plus,
                 model_next, answer, wide, cross, picked):
    cells = gu * gv
    slots, columns = rows.shape
    half = columns // 2

    chunk = 512

    @pl.loop(0, cells // chunk)
    def _(i):
        at = pl.ds(pl.multiple_of(i * chunk, chunk), chunk)
        wide[at, :] = jnp.zeros((chunk, columns), jnp.float32)
        cross[at, :] = panel[at, :].astype(jnp.float32)

    wide[pl.ds(cells, 8), :] = jnp.zeros((8, columns), jnp.float32)

    @pl.loop(0, slots // 16)
    def _(i):
        base = pl.multiple_of(i * 16, 16)
        for k in range(16):
            picked[pl.ds(base + k, 1), :] = cross[pl.ds(panel_at[base + k], 1), :]

    lane = lax.broadcasted_iota(jnp.int32, (slots, columns), 1)
    kernel_rows = picked[...]
    swapped = pltpu.roll(kernel_rows, half, 1)
    real = jnp.where(lane < half, kernel_rows, swapped)
    imag = jnp.where(lane < half, swapped, kernel_rows)
    values = rows[...].astype(jnp.float32)
    cross[pl.ds(0, slots), :] = values * real + turned(values) * imag

    @pl.loop(0, slots // 16)
    def _(i):
        base = pl.multiple_of(i * 16, 16)
        for k in range(16):
            at = pl.ds(grid_at[base + k], 1)
            wide[at, :] += cross[pl.ds(base + k, 1), :]

    @pl.loop(0, gv // GROUP, unroll=UNROLL)
    def _(i):
        base = pl.multiple_of(i * (GROUP * gu), GROUP * gu)
        out = stage(minus[...], [wide[pl.ds(base + k * gu, gu), :] for k in range(GROUP)])
        for k in range(GROUP):
            cross[pl.ds(GROUP * i + k, gu, stride=gv), :] = out[k]

    gain = scale[0]

    @pl.loop(0, gu // GROUP, unroll=UNROLL)
    def _(i):
        base = pl.multiple_of(i * (GROUP * gv), GROUP * gv)
        at = [pl.ds(base + k * gv, gv) for k in range(GROUP)]
        out = stage(minus[...], [cross[here, :] for here in at])
        updated = []
        for k in range(GROUP):
            value = (model[at[k], :].astype(jnp.float32) + gain * out[k]).astype(jnp.bfloat16)
            model_next[at[k], :] = value
            updated.append(value.astype(jnp.float32))
        out = stage(plus[...], updated)
        for k in range(GROUP):
            wide[pl.ds(GROUP * i + k, gv, stride=gu), :] = out[k]

    @pl.loop(0, gv // GROUP, unroll=UNROLL)
    def _(i):
        base = pl.multiple_of(i * (GROUP * gu), GROUP * gu)
        out = stage(plus[...], [wide[pl.ds(base + k * gu, gu), :] for k in range(GROUP)])
        for k in range(GROUP):
            cross[pl.ds(base + k * gu, gu), :] = out[k]

    cross[pl.ds(cells, 8), :] = jnp.zeros((8, columns), jnp.float32)

    @pl.loop(0, slots // 16)
    def _(i):
        base = pl.multiple_of(i * 16, 16)
        for k in range(16):
            wide[pl.ds(base + k, 1), :] = cross[pl.ds(grid_at[base + k], 1), :]

    kernel_rows = picked[...]
    swapped = pltpu.roll(kernel_rows, half, 1)
    real = jnp.where(lane < half, kernel_rows, swapped)
    imag = jnp.where(lane < half, swapped, kernel_rows)
    found = wide[pl.ds(0, slots), :] * (1.0 / math.sqrt(cells))
    predicted = found * real - turned(found) * imag
    answer[...] = (rows[...].astype(jnp.float32) - predicted).astype(jnp.bfloat16)


def run_cycle(gu, gv, grid_at, panel_at, scale, rows, panel, model):
    cells = gu * gv
    slots, columns = rows.shape
    smem = pl.BlockSpec(memory_space=pltpu.SMEM)
    vmem = pl.BlockSpec(memory_space=pltpu.VMEM)
    return pl.pallas_call(
        functools.partial(cycle_kernel, gu, gv),
        out_shape=(
            jax.ShapeDtypeStruct((cells, columns), jnp.bfloat16),
            jax.ShapeDtypeStruct((slots, columns), jnp.bfloat16),
        ),
        in_specs=[smem] * 3 + [vmem] * 5,
        out_specs=(vmem, vmem),
        scratch_shapes=[
            pltpu.VMEM((cells + 8, columns), jnp.float32),
            pltpu.VMEM((cells + 8, columns), jnp.float32),
            pltpu.VMEM((slots, columns), jnp.float32),
        ],
        compiler_params=pltpu.CompilerParams(vmem_limit_bytes=50 * 1024 * 1024),
    )(grid_at, panel_at, scale, rows, panel, model, dft_table(gu, -1), dft_table(gu, 1))


def greet(peers):
    me = lax.axis_index("facet")
    barrier = pltpu.get_barrier_semaphore()
    for step in range(1, peers):
        pl.semaphore_signal(
            barrier, inc=1, device_id={"facet": lax.rem(me + step, peers)}, device_id_type=MESH
        )
    pl.semaphore_wait(barrier, peers - 1)


def sent(source, target, send_sem, recv_sem, peer):
    copy = pltpu.make_async_remote_copy(
        src_ref=source, dst_ref=target, send_sem=send_sem, recv_sem=recv_sem,
        device_id={"facet": peer}, device_id_type=MESH,
    )
    copy.start()
    return copy


def swap_blocks(peers, source, target, send_sems, recv_sems):
    me = lax.axis_index("facet")
    copies = []
    for step in range(1, peers):
        peer = lax.rem(me + step, peers)
        copies.append(
            sent(source.at[peer], target.at[me], send_sems.at[step], recv_sems.at[step], peer)
        )
    return copies


def chip_at(place, chips):
    if chips != 8:
        return place
    back = place // 4
    return (1 - back) * (2 * place) + back * (15 - 2 * place)


def place_of(chip, chips):
    if chips != 8:
        return chip
    return chip // 2 + (chip % 2) * (7 - 2 * (chip // 2))


def spread_kernel(peers, rows, ids, taper, rows_out, ids_out, panel, own_sems, row_send, row_recv,
                  id_send, id_recv, ring_send, ring_recv, pass_send, pass_recv):
    me = lax.axis_index("facet")
    chips = peers // 2
    core, place = lax.rem(me, 2), place_of(me // 2, chips)
    sibling = me + 1 - 2 * core
    depth = taper.shape[0]
    half = depth // 2

    def owner(distance):
        return chip_at(lax.rem(place + distance + chips, chips), chips) * 2 + core

    right, left = owner(1), owner(-1)
    greet(peers)

    own = [
        pltpu.make_async_copy(rows.at[me], rows_out.at[me], own_sems.at[0]),
        pltpu.make_async_copy(ids.at[me], ids_out.at[me], own_sems.at[1]),
        pltpu.make_async_copy(taper, panel.at[me], own_sems.at[2]),
    ]

    def ring(way, step, peer):
        if step == 0:
            source, target = taper, panel.at[me]
        else:
            block = owner(-step if way == 0 else step)
            source = target = panel.at[block]
            if step == chips // 2 - 1:
                part = pl.ds(way * half, half)
                source = target = panel.at[block, part]
        return sent(source, target, ring_send.at[way, step], ring_recv.at[way, step], peer)

    started = []
    going = [ring(0, 0, right), ring(1, 0, left)]
    moves = swap_blocks(peers, ids, ids_out, id_send, id_recv)
    moves += swap_blocks(peers, rows, rows_out, row_send, row_recv)
    passed = [sent(taper, panel.at[me], pass_send.at[0, 0], pass_recv.at[0, 0], sibling)]
    for copy in own:
        copy.start()
    for step in range(chips // 2):
        arrived = going
        started += going
        going = []
        for way in range(2):
            arrived[way].wait_recv()
            if step + 1 < chips // 2:
                going.append(ring(way, step + 1, right if way == 0 else left))
            block = owner(-(step + 1) if way == 0 else step + 1)
            fresh = panel.at[block]
            if step == chips // 2 - 1:
                fresh = panel.at[block, pl.ds(way * half, half)]
            at = (way, step + 1)
            passed.append(sent(fresh, fresh, pass_send.at[at], pass_recv.at[at], sibling))
    for copy in started:
        copy.wait_send()
    for copy in moves + passed:
        copy.wait()
    for copy in own:
        copy.wait()


def spread(peers, rows, ids, taper):
    steps = peers // 4
    hbm = pl.BlockSpec(memory_space=pl.ANY)
    dma = pltpu.SemaphoreType.DMA
    return pl.pallas_call(
        functools.partial(spread_kernel, peers),
        out_shape=(
            jax.ShapeDtypeStruct(rows.shape, rows.dtype),
            jax.ShapeDtypeStruct(ids.shape, ids.dtype),
            jax.ShapeDtypeStruct((peers,) + taper.shape, taper.dtype),
        ),
        in_specs=[hbm] * 3,
        out_specs=(hbm,) * 3,
        scratch_shapes=[dma((3,))] + [dma((peers,))] * 4 + [dma((2, steps))] * 2
        + [dma((2, steps + 1))] * 2,
        compiler_params=pltpu.CompilerParams(collective_id=0, has_side_effects=True),
    )(rows, ids, taper)


def back_kernel(peers, answer, returned, own_sem, send_sems, recv_sems):
    me = lax.axis_index("facet")
    own = pltpu.make_async_copy(answer.at[me], returned.at[me], own_sem)
    own.start()
    greet(peers)
    for copy in swap_blocks(peers, answer, returned, send_sems, recv_sems):
        copy.wait()
    own.wait()


def send_back(peers, answer):
    hbm = pl.BlockSpec(memory_space=pl.ANY)
    dma = pltpu.SemaphoreType.DMA
    return pl.pallas_call(
        functools.partial(back_kernel, peers),
        out_shape=jax.ShapeDtypeStruct(answer.shape, answer.dtype),
        in_specs=[hbm],
        out_specs=hbm,
        scratch_shapes=[dma, dma((peers,)), dma((peers,))],
        compiler_params=pltpu.CompilerParams(collective_id=1, has_side_effects=True),
    )(answer)


def body(visibility, facet_of, cell_of, taper, model):
    peers = lax.axis_size("facet")
    local_rows, columns = visibility.shape
    capacity = 2 * local_rows // peers
    slots = peers * capacity
    cells = model.shape[0]
    gu = gv = math.isqrt(cells)

    target = facet_of[:, 0]
    order = jnp.arange(local_rows, dtype=jnp.int32)
    earlier = (order[:, None] > order[None, :]) & (target[:, None] == target[None, :])
    position = target * capacity + jnp.sum(earlier.astype(jnp.int32), axis=1)
    placed = jnp.arange(slots, dtype=jnp.int32)[:, None] == position[None, :]
    send_rows = jnp.dot(
        placed.astype(jnp.bfloat16), visibility, preferred_element_type=jnp.float32
    ).astype(jnp.bfloat16)
    send_cells = jnp.min(jnp.where(placed, cell_of[None, :], cells), axis=1)

    ids = jnp.pad(send_cells.reshape(peers, 1, capacity), ((0, 0), (0, 7), (0, 128 - capacity)))
    rows, ids, panel = spread(peers, send_rows.reshape(peers, capacity, columns), ids, taper)
    rows = rows.reshape(slots, columns)
    panel = panel.reshape(cells, columns)
    cell_ids = ids[:, 0, :capacity].reshape(slots)

    used = cell_ids < cells
    scale = LOOP_GAIN / jnp.sqrt(jnp.sum(used.astype(jnp.float32)))
    grid_at = jnp.where(used, cell_ids % gv * gu + cell_ids // gv, cells)
    panel_at = jnp.minimum(cell_ids, cells - 1)
    model_next, answer = run_cycle(gu, gv, grid_at, panel_at, scale.reshape(1), rows, panel, model)

    returned = send_back(peers, answer.reshape(peers, capacity, columns)).reshape(slots, columns)
    residual = lax.dot_general(
        placed.astype(jnp.bfloat16), returned, (((0,), (0,)), ((), ())),
        preferred_element_type=jnp.float32,
    ).astype(jnp.bfloat16)
    return (model_next, residual)


def solution(mesh):
    both = ("groups", "facet")
    return jax.shard_map(
        body,
        mesh=mesh,
        in_specs=(P(both, None), P(both, None), P(both), P(both, None), P(both, None)),
        out_specs=(P(both, None), P(both, None)),
        check_vma=False,
    )
```

```python
import functools
import math

import jax
import jax.numpy as jnp
from jax import lax
from jax.experimental import pallas as pl
from jax.experimental.pallas import tpu as pltpu
from jax.sharding import PartitionSpec as P

LOOP_GAIN = 0.1
MESH = pl.DeviceIdType.MESH
GROUP = 8
UNROLL = 2


def dft_table(length, orient):
    ordinal = jnp.arange(length, dtype=jnp.int32)
    phases = ordinal[:, None] * ordinal[None, :] % length
    angles = phases.astype(jnp.float32) * (2.0 * math.pi / length)
    return jnp.concatenate([jnp.cos(angles), orient * jnp.sin(angles)], 1).astype(jnp.bfloat16)


def turned(values):
    half = values.shape[-1] // 2
    lane = lax.broadcasted_iota(jnp.int32, values.shape, 1)
    rolled = pltpu.roll(values, half, 1)
    return jnp.where(lane < half, -rolled, rolled)


def stage(table, slabs):
    columns = slabs[0].shape[1]
    top = jnp.concatenate(slabs, 1).astype(jnp.bfloat16)
    low = jnp.concatenate([turned(slab) for slab in slabs], 1).astype(jnp.bfloat16)
    out = jnp.dot(table, jnp.concatenate([top, low], 0), preferred_element_type=jnp.float32)
    return [out[:, k * columns : (k + 1) * columns] for k in range(len(slabs))]


def cycle_kernel(gu, gv, capacity, ids, rows, panel_in, model_in, minus, plus,
                 model_next, answer, wide, cross, picked, panel, model, sems):
    cells = gu * gv
    slots, columns = rows.shape
    half = columns // 2
    runs = capacity // 16
    bits = gu.bit_length() - 1
    assert gu == gv == 1 << bits
    panel_copy = pltpu.make_async_copy(panel_in, panel, sems.at[0])
    model_copy = pltpu.make_async_copy(model_in, model, sems.at[1])
    panel_copy.start()
    model_copy.start()

    def grid_at(i, k):
        return ids[lax.div(i, runs), 0, lax.rem(i, runs) * 16 + k]

    chunk = 512

    @pl.loop(0, cells // chunk)
    def _(i):
        at = pl.ds(pl.multiple_of(i * chunk, chunk), chunk)
        wide[at, :] = jnp.zeros((chunk, columns), jnp.float32)

    panel_copy.wait()

    @pl.loop(0, cells // chunk)
    def _(i):
        at = pl.ds(pl.multiple_of(i * chunk, chunk), chunk)
        cross[at, :] = panel[at, :].astype(jnp.float32)

    wide[pl.ds(cells, 8), :] = jnp.zeros((8, columns), jnp.float32)

    def pick(i, used):
        base = pl.multiple_of(i * 16, 16)
        for k in range(16):
            here = grid_at(i, k)
            used += (here < cells).astype(jnp.int32)
            here = jnp.minimum(here, cells - 1)
            picked[pl.ds(base + k, 1), :] = cross[pl.ds(((here & (gu - 1)) << bits) + (here >> bits), 1), :]
        return used

    used = lax.fori_loop(0, slots // 16, pick, jnp.int32(0))

    lane = lax.broadcasted_iota(jnp.int32, (slots, columns), 1)
    kernel_rows = picked[...]
    swapped = pltpu.roll(kernel_rows, half, 1)
    real = jnp.where(lane < half, kernel_rows, swapped)
    imag = jnp.where(lane < half, swapped, kernel_rows)
    values = rows[...].astype(jnp.float32)
    cross[pl.ds(0, slots), :] = values * real + turned(values) * imag

    @pl.loop(0, slots // 16)
    def _(i):
        base = pl.multiple_of(i * 16, 16)
        for k in range(16):
            at = pl.ds(grid_at(i, k), 1)
            wide[at, :] += cross[pl.ds(base + k, 1), :]

    @pl.loop(0, gv // GROUP, unroll=UNROLL)
    def _(i):
        base = pl.multiple_of(i * (GROUP * gu), GROUP * gu)
        out = stage(minus[...], [wide[pl.ds(base + k * gu, gu), :] for k in range(GROUP)])
        for k in range(GROUP):
            cross[pl.ds(GROUP * i + k, gu, stride=gv), :] = out[k]

    count = jnp.full((1, columns), used, jnp.int32).astype(jnp.float32)
    gain = LOOP_GAIN / jnp.sqrt(count)
    model_copy.wait()

    @pl.loop(0, gu // GROUP, unroll=UNROLL)
    def _(i):
        base = pl.multiple_of(i * (GROUP * gv), GROUP * gv)
        at = [pl.ds(base + k * gv, gv) for k in range(GROUP)]
        out = stage(minus[...], [cross[here, :] for here in at])
        updated = []
        for k in range(GROUP):
            value = (model[at[k], :].astype(jnp.float32) + gain * out[k]).astype(jnp.bfloat16)
            model[at[k], :] = value
            updated.append(value.astype(jnp.float32))
        out = stage(plus[...], updated)
        for k in range(GROUP):
            wide[pl.ds(GROUP * i + k, gv, stride=gu), :] = out[k]

    next_copy = pltpu.make_async_copy(model, model_next, sems.at[2])
    next_copy.start()

    @pl.loop(0, gv // GROUP, unroll=UNROLL)
    def _(i):
        base = pl.multiple_of(i * (GROUP * gu), GROUP * gu)
        out = stage(plus[...], [wide[pl.ds(base + k * gu, gu), :] for k in range(GROUP)])
        for k in range(GROUP):
            cross[pl.ds(base + k * gu, gu), :] = out[k]

    cross[pl.ds(cells, 8), :] = jnp.zeros((8, columns), jnp.float32)

    @pl.loop(0, slots // 16)
    def _(i):
        base = pl.multiple_of(i * 16, 16)
        for k in range(16):
            wide[pl.ds(base + k, 1), :] = cross[pl.ds(grid_at(i, k), 1), :]

    kernel_rows = picked[...]
    swapped = pltpu.roll(kernel_rows, half, 1)
    real = jnp.where(lane < half, kernel_rows, swapped)
    imag = jnp.where(lane < half, swapped, kernel_rows)
    found = wide[pl.ds(0, slots), :] * (1.0 / math.sqrt(cells))
    predicted = found * real - turned(found) * imag
    answer[...] = (rows[...].astype(jnp.float32) - predicted).astype(jnp.bfloat16)
    next_copy.wait()


def run_cycle(gu, gv, ids, rows, panel, model):
    cells = gu * gv
    slots, columns = rows.shape
    smem = pl.BlockSpec(memory_space=pltpu.SMEM)
    vmem = pl.BlockSpec(memory_space=pltpu.VMEM)
    hbm = pl.BlockSpec(memory_space=pl.ANY)
    return pl.pallas_call(
        functools.partial(cycle_kernel, gu, gv, slots // ids.shape[0]),
        out_shape=(
            jax.ShapeDtypeStruct((cells, columns), jnp.bfloat16),
            jax.ShapeDtypeStruct((slots, columns), jnp.bfloat16),
        ),
        in_specs=[smem, vmem, hbm, hbm, vmem, vmem],
        out_specs=(hbm, vmem),
        scratch_shapes=[
            pltpu.VMEM((cells + 8, columns), jnp.float32),
            pltpu.VMEM((cells + 8, columns), jnp.float32),
            pltpu.VMEM((slots, columns), jnp.float32),
            pltpu.VMEM((cells, columns), jnp.bfloat16),
            pltpu.VMEM((cells, columns), jnp.bfloat16),
            pltpu.SemaphoreType.DMA((3,)),
        ],
        compiler_params=pltpu.CompilerParams(vmem_limit_bytes=50 * 1024 * 1024),
    )(ids, rows, panel, model, dft_table(gu, -1), dft_table(gu, 1))


def greet(peers):
    me = lax.axis_index("facet")
    barrier = pltpu.get_barrier_semaphore()
    for step in range(1, peers):
        pl.semaphore_signal(
            barrier, inc=1, device_id={"facet": lax.rem(me + step, peers)}, device_id_type=MESH
        )
    pl.semaphore_wait(barrier, peers - 1)


def sent(source, target, send_sem, recv_sem, peer):
    copy = pltpu.make_async_remote_copy(
        src_ref=source, dst_ref=target, send_sem=send_sem, recv_sem=recv_sem,
        device_id={"facet": peer}, device_id_type=MESH,
    )
    copy.start()
    return copy


def swap_blocks(peers, source, target, send_sems, recv_sems):
    me = lax.axis_index("facet")
    copies = []
    for step in range(1, peers):
        peer = lax.rem(me + step, peers)
        copies.append(
            sent(source.at[peer], target.at[me], send_sems.at[step], recv_sems.at[step], peer)
        )
    return copies


def chip_at(place, chips):
    if chips != 8:
        return place
    back = place // 4
    return (1 - back) * (2 * place) + back * (15 - 2 * place)


def place_of(chip, chips):
    if chips != 8:
        return chip
    return chip // 2 + (chip % 2) * (7 - 2 * (chip // 2))


def spread_kernel(peers, rows, ids, taper, rows_out, ids_out, panel, own_sems, row_send, row_recv,
                  id_send, id_recv, ring_send, ring_recv, pass_send, pass_recv):
    me = lax.axis_index("facet")
    chips = peers // 2
    core, place = lax.rem(me, 2), place_of(me // 2, chips)
    sibling = me + 1 - 2 * core
    depth = taper.shape[0]
    half = depth // 2

    def owner(distance):
        return chip_at(lax.rem(place + distance + chips, chips), chips) * 2 + core

    right, left = owner(1), owner(-1)
    greet(peers)

    own = [
        pltpu.make_async_copy(rows.at[me], rows_out.at[me], own_sems.at[0]),
        pltpu.make_async_copy(ids.at[me], ids_out.at[me], own_sems.at[1]),
        pltpu.make_async_copy(taper, panel.at[me], own_sems.at[2]),
    ]

    def goes(way, step, piece):
        return step < chips // 2 - 1 or (step == chips // 2 - 1 and piece == way)

    def ring(way, step, piece):
        part = pl.ds(piece * half, half)
        block = owner(-step if way == 0 else step)
        source = taper.at[part] if step == 0 else panel.at[block, part]
        at = (way, step, piece)
        peer = right if way == 0 else left
        return sent(source, panel.at[block, part], ring_send.at[at], ring_recv.at[at], peer)

    started = {}
    for piece in range(2):
        for way in range(2):
            started[way, 0, piece] = ring(way, 0, piece)
    moves = swap_blocks(peers, ids, ids_out, id_send, id_recv)
    moves += swap_blocks(peers, rows, rows_out, row_send, row_recv)
    passed = [sent(taper, panel.at[me], pass_send.at[0, 0, 0], pass_recv.at[0, 0, 0], sibling)]
    for copy in own:
        copy.start()
    for step in range(chips // 2):
        for piece in range(2):
            for way in range(2):
                if not goes(way, step, piece):
                    continue
                started[way, step, piece].wait_recv()
                if goes(way, step + 1, piece):
                    started[way, step + 1, piece] = ring(way, step + 1, piece)
                block = owner(-(step + 1) if way == 0 else step + 1)
                fresh = panel.at[block, pl.ds(piece * half, half)]
                at = (way, step + 1, piece)
                passed.append(sent(fresh, fresh, pass_send.at[at], pass_recv.at[at], sibling))
    for copy in started.values():
        copy.wait_send()
    for copy in moves + passed:
        copy.wait()
    for copy in own:
        copy.wait()


def spread(peers, rows, ids, taper):
    steps = peers // 4
    hbm = pl.BlockSpec(memory_space=pl.ANY)
    dma = pltpu.SemaphoreType.DMA
    return pl.pallas_call(
        functools.partial(spread_kernel, peers),
        out_shape=(
            jax.ShapeDtypeStruct(rows.shape, rows.dtype),
            jax.ShapeDtypeStruct(ids.shape, ids.dtype),
            jax.ShapeDtypeStruct((peers,) + taper.shape, taper.dtype),
        ),
        in_specs=[hbm] * 3,
        out_specs=(hbm,) * 3,
        scratch_shapes=[dma((3,))] + [dma((peers,))] * 4 + [dma((2, steps, 2))] * 2
        + [dma((2, steps + 1, 2))] * 2,
        compiler_params=pltpu.CompilerParams(collective_id=0, has_side_effects=True),
    )(rows, ids, taper)


def back_kernel(peers, answer, returned, own_sem, send_sems, recv_sems):
    me = lax.axis_index("facet")
    own = pltpu.make_async_copy(answer.at[me], returned.at[me], own_sem)
    own.start()
    greet(peers)
    for copy in swap_blocks(peers, answer, returned, send_sems, recv_sems):
        copy.wait()
    own.wait()


def send_back(peers, answer):
    hbm = pl.BlockSpec(memory_space=pl.ANY)
    dma = pltpu.SemaphoreType.DMA
    return pl.pallas_call(
        functools.partial(back_kernel, peers),
        out_shape=jax.ShapeDtypeStruct(answer.shape, answer.dtype),
        in_specs=[hbm],
        out_specs=hbm,
        scratch_shapes=[dma, dma((peers,)), dma((peers,))],
        compiler_params=pltpu.CompilerParams(collective_id=1, has_side_effects=True),
    )(answer)


def body(visibility, facet_of, cell_of, taper, model):
    peers = lax.axis_size("facet")
    local_rows, columns = visibility.shape
    capacity = 2 * local_rows // peers
    slots = peers * capacity
    cells = model.shape[0]
    gu = gv = math.isqrt(cells)

    target = facet_of[:, 0]
    order = jnp.arange(local_rows, dtype=jnp.int32)
    earlier = (order[:, None] > order[None, :]) & (target[:, None] == target[None, :])
    position = target * capacity + jnp.sum(earlier.astype(jnp.int32), axis=1)
    placed = jnp.arange(slots, dtype=jnp.int32)[:, None] == position[None, :]
    send_rows = jnp.dot(
        placed.astype(jnp.bfloat16), visibility, preferred_element_type=jnp.float32
    ).astype(jnp.bfloat16)
    turned_cell = cell_of % gv * gu + cell_of // gv
    send_cells = jnp.min(jnp.where(placed, turned_cell[None, :], cells), axis=1)

    ids = jnp.pad(send_cells.reshape(peers, 1, capacity), ((0, 0), (0, 7), (0, 128 - capacity)))
    rows, ids, panel = spread(peers, send_rows.reshape(peers, capacity, columns), ids, taper)
    rows = rows.reshape(slots, columns)
    panel = panel.reshape(cells, columns)
    model_next, answer = run_cycle(gu, gv, ids, rows, panel, model)

    returned = send_back(peers, answer.reshape(peers, capacity, columns)).reshape(slots, columns)
    residual = lax.dot_general(
        placed.astype(jnp.bfloat16), returned, (((0,), (0,)), ((), ())),
        preferred_element_type=jnp.float32,
    ).astype(jnp.bfloat16)
    return (model_next, residual)


def solution(mesh):
    both = ("groups", "facet")
    return jax.shard_map(
        body,
        mesh=mesh,
        in_specs=(P(both, None), P(both, None), P(both), P(both, None), P(both, None)),
        out_specs=(P(both, None), P(both, None)),
        check_vma=False,
    )
```

```python
import functools
import math

import jax
import jax.numpy as jnp
from jax import lax
from jax.experimental import pallas as pl
from jax.experimental.pallas import tpu as pltpu
from jax.sharding import PartitionSpec as P

LOOP_GAIN = 0.1
MESH = pl.DeviceIdType.MESH
GROUP = 16
UNROLL = 2
PAD = 8


def dft_table(length, orient):
    ordinal = jnp.arange(length, dtype=jnp.int32)
    phases = ordinal[:, None] * ordinal[None, :] % length
    angles = phases.astype(jnp.float32) * (2.0 * math.pi / length)
    return jnp.concatenate([jnp.cos(angles), orient * jnp.sin(angles)], 1).astype(jnp.bfloat16)


def turned(values):
    half = values.shape[-1] // 2
    lane = lax.broadcasted_iota(jnp.int32, values.shape, 1)
    rolled = pltpu.roll(values, half, 1)
    return jnp.where(lane < half, -rolled, rolled)


def stage(table, slabs):
    columns = slabs[0].shape[1]
    top = jnp.concatenate(slabs, 1).astype(jnp.bfloat16)
    low = jnp.concatenate([turned(slab) for slab in slabs], 1).astype(jnp.bfloat16)
    out = jnp.dot(table, jnp.concatenate([top, low], 0), preferred_element_type=jnp.float32)
    return [out[:, k * columns : (k + 1) * columns] for k in range(len(slabs))]


def cycle_kernel(gu, gv, capacity, ids, rows, panel_in, model_in, minus, plus,
                 model_next, answer, wide, cross, picked, panel, model, sems):
    cells = gu * gv
    slots, columns = rows.shape
    half = columns // 2
    runs = capacity // 16
    bits = gu.bit_length() - 1
    assert gu == gv == 1 << bits
    panel_copy = pltpu.make_async_copy(panel_in, panel, sems.at[0])
    model_copy = pltpu.make_async_copy(model_in, model, sems.at[1])
    panel_copy.start()
    model_copy.start()

    def grid_at(i, k):
        return ids[lax.div(i, runs), 0, lax.rem(i, runs) * 16 + k]

    chunk = 512

    @pl.loop(0, cells // chunk)
    def _(i):
        at = pl.ds(pl.multiple_of(i * chunk, chunk), chunk)
        wide[at, :] = jnp.zeros((chunk, columns), jnp.float32)

    panel_copy.wait()

    @pl.loop(0, cells // chunk)
    def _(i):
        at = pl.ds(pl.multiple_of(i * chunk, chunk), chunk)
        cross[at, :] = panel[at, :].astype(jnp.float32)

    wide[pl.ds(cells, 8), :] = jnp.zeros((8, columns), jnp.float32)

    def pick(i, used):
        base = pl.multiple_of(i * 16, 16)
        for k in range(16):
            here = grid_at(i, k)
            used += (here < cells).astype(jnp.int32)
            here = jnp.minimum(here, cells - 1)
            picked[pl.ds(base + k, 1), :] = cross[pl.ds(((here & (gu - 1)) << bits) + (here >> bits), 1), :]
        return used

    used = lax.fori_loop(0, slots // 16, pick, jnp.int32(0))

    lane = lax.broadcasted_iota(jnp.int32, (slots, columns), 1)
    kernel_rows = picked[...]
    swapped = pltpu.roll(kernel_rows, half, 1)
    real = jnp.where(lane < half, kernel_rows, swapped)
    imag = jnp.where(lane < half, swapped, kernel_rows)
    values = rows[...].astype(jnp.float32)
    cross[pl.ds(0, slots), :] = values * real + turned(values) * imag

    @pl.loop(0, slots // 16)
    def _(i):
        base = pl.multiple_of(i * 16, 16)
        for k in range(16):
            at = pl.ds(grid_at(i, k), 1)
            wide[at, :] += cross[pl.ds(base + k, 1), :]

    @pl.loop(0, gv // GROUP, unroll=UNROLL)
    def _(i):
        base = pl.multiple_of(i * (GROUP * gu), GROUP * gu)
        out = stage(minus[...], [wide[pl.ds(base + k * gu, gu), :] for k in range(GROUP)])
        for k in range(GROUP):
            cross[pl.ds(GROUP * i + k, gu, stride=gv + PAD), :] = out[k]

    count = jnp.full((1, columns), used, jnp.int32).astype(jnp.float32)
    gain = LOOP_GAIN / jnp.sqrt(count)
    model_copy.wait()

    @pl.loop(0, gu // GROUP, unroll=UNROLL)
    def _(i):
        base = pl.multiple_of(i * (GROUP * gv), GROUP * gv)
        at = [pl.ds(base + k * gv, gv) for k in range(GROUP)]
        apart = pl.multiple_of(i * (GROUP * (gv + PAD)), 8)
        out = stage(minus[...], [cross[pl.ds(apart + k * (gv + PAD), gv), :] for k in range(GROUP)])
        updated = []
        for k in range(GROUP):
            value = (model[at[k], :].astype(jnp.float32) + gain * out[k]).astype(jnp.bfloat16)
            model[at[k], :] = value
            updated.append(value.astype(jnp.float32))
        out = stage(plus[...], updated)
        for k in range(GROUP):
            wide[pl.ds(GROUP * i + k, gv, stride=gu + PAD), :] = out[k]

    next_copy = pltpu.make_async_copy(model, model_next, sems.at[2])
    next_copy.start()

    @pl.loop(0, gv // GROUP, unroll=UNROLL)
    def _(i):
        base = pl.multiple_of(i * (GROUP * gu), GROUP * gu)
        apart = pl.multiple_of(i * (GROUP * (gu + PAD)), 8)
        out = stage(plus[...], [wide[pl.ds(apart + k * (gu + PAD), gu), :] for k in range(GROUP)])
        for k in range(GROUP):
            cross[pl.ds(base + k * gu, gu), :] = out[k]

    cross[pl.ds(cells, 8), :] = jnp.zeros((8, columns), jnp.float32)

    @pl.loop(0, slots // 16)
    def _(i):
        base = pl.multiple_of(i * 16, 16)
        for k in range(16):
            wide[pl.ds(base + k, 1), :] = cross[pl.ds(grid_at(i, k), 1), :]

    kernel_rows = picked[...]
    swapped = pltpu.roll(kernel_rows, half, 1)
    real = jnp.where(lane < half, kernel_rows, swapped)
    imag = jnp.where(lane < half, swapped, kernel_rows)
    found = wide[pl.ds(0, slots), :] * (1.0 / math.sqrt(cells))
    predicted = found * real - turned(found) * imag
    answer[...] = (rows[...].astype(jnp.float32) - predicted).astype(jnp.bfloat16)
    next_copy.wait()


def run_cycle(gu, gv, ids, rows, panel, model):
    cells = gu * gv
    slots, columns = rows.shape
    smem = pl.BlockSpec(memory_space=pltpu.SMEM)
    vmem = pl.BlockSpec(memory_space=pltpu.VMEM)
    hbm = pl.BlockSpec(memory_space=pl.ANY)
    return pl.pallas_call(
        functools.partial(cycle_kernel, gu, gv, slots // ids.shape[0]),
        out_shape=(
            jax.ShapeDtypeStruct((cells, columns), jnp.bfloat16),
            jax.ShapeDtypeStruct((slots, columns), jnp.bfloat16),
        ),
        in_specs=[smem, vmem, hbm, hbm, vmem, vmem],
        out_specs=(hbm, vmem),
        scratch_shapes=[
            pltpu.VMEM((gv * (gu + PAD) + 8, columns), jnp.float32),
            pltpu.VMEM((gu * (gv + PAD) + 8, columns), jnp.float32),
            pltpu.VMEM((slots, columns), jnp.float32),
            pltpu.VMEM((cells, columns), jnp.bfloat16),
            pltpu.VMEM((cells, columns), jnp.bfloat16),
            pltpu.SemaphoreType.DMA((3,)),
        ],
        compiler_params=pltpu.CompilerParams(vmem_limit_bytes=50 * 1024 * 1024),
    )(ids, rows, panel, model, dft_table(gu, -1), dft_table(gu, 1))


def greet(peers):
    me = lax.axis_index("facet")
    barrier = pltpu.get_barrier_semaphore()
    for step in range(1, peers):
        pl.semaphore_signal(
            barrier, inc=1, device_id={"facet": lax.rem(me + step, peers)}, device_id_type=MESH
        )
    pl.semaphore_wait(barrier, peers - 1)


def sent(source, target, send_sem, recv_sem, peer):
    copy = pltpu.make_async_remote_copy(
        src_ref=source, dst_ref=target, send_sem=send_sem, recv_sem=recv_sem,
        device_id={"facet": peer}, device_id_type=MESH,
    )
    copy.start()
    return copy


def swap_blocks(peers, source, target, send_sems, recv_sems):
    me = lax.axis_index("facet")
    copies = []
    for step in range(1, peers):
        peer = lax.rem(me + step, peers)
        copies.append(
            sent(source.at[peer], target.at[me], send_sems.at[step], recv_sems.at[step], peer)
        )
    return copies


def chip_at(place, chips):
    if chips != 8:
        return place
    back = place // 4
    return (1 - back) * (2 * place) + back * (15 - 2 * place)


def place_of(chip, chips):
    if chips != 8:
        return chip
    return chip // 2 + (chip % 2) * (7 - 2 * (chip // 2))


def spread_kernel(peers, rows, ids, taper, rows_out, ids_out, panel, own_sems, row_send, row_recv,
                  id_send, id_recv, ring_send, ring_recv, pass_send, pass_recv):
    me = lax.axis_index("facet")
    chips = peers // 2
    core, place = lax.rem(me, 2), place_of(me // 2, chips)
    sibling = me + 1 - 2 * core
    depth = taper.shape[0]
    half = depth // 2

    def owner(distance):
        return chip_at(lax.rem(place + distance + chips, chips), chips) * 2 + core

    right, left = owner(1), owner(-1)
    greet(peers)

    own = [
        pltpu.make_async_copy(rows.at[me], rows_out.at[me], own_sems.at[0]),
        pltpu.make_async_copy(ids.at[me], ids_out.at[me], own_sems.at[1]),
        pltpu.make_async_copy(taper, panel.at[me], own_sems.at[2]),
    ]

    def goes(way, step, piece):
        return step < chips // 2 - 1 or (step == chips // 2 - 1 and piece == way)

    def ring(way, step, piece):
        part = pl.ds(piece * half, half)
        block = owner(-step if way == 0 else step)
        source = taper.at[part] if step == 0 else panel.at[block, part]
        at = (way, step, piece)
        peer = right if way == 0 else left
        return sent(source, panel.at[block, part], ring_send.at[at], ring_recv.at[at], peer)

    started = {}
    for piece in range(2):
        for way in range(2):
            started[way, 0, piece] = ring(way, 0, piece)
    moves = swap_blocks(peers, ids, ids_out, id_send, id_recv)
    moves += swap_blocks(peers, rows, rows_out, row_send, row_recv)
    passed = [sent(taper, panel.at[me], pass_send.at[0, 0, 0], pass_recv.at[0, 0, 0], sibling)]
    for copy in own:
        copy.start()
    for step in range(chips // 2):
        for piece in range(2):
            for way in range(2):
                if not goes(way, step, piece):
                    continue
                started[way, step, piece].wait_recv()
                if goes(way, step + 1, piece):
                    started[way, step + 1, piece] = ring(way, step + 1, piece)
                block = owner(-(step + 1) if way == 0 else step + 1)
                fresh = panel.at[block, pl.ds(piece * half, half)]
                at = (way, step + 1, piece)
                passed.append(sent(fresh, fresh, pass_send.at[at], pass_recv.at[at], sibling))
    for copy in started.values():
        copy.wait_send()
    for copy in moves + passed:
        copy.wait()
    for copy in own:
        copy.wait()


def spread(peers, rows, ids, taper):
    steps = peers // 4
    hbm = pl.BlockSpec(memory_space=pl.ANY)
    dma = pltpu.SemaphoreType.DMA
    return pl.pallas_call(
        functools.partial(spread_kernel, peers),
        out_shape=(
            jax.ShapeDtypeStruct(rows.shape, rows.dtype),
            jax.ShapeDtypeStruct(ids.shape, ids.dtype),
            jax.ShapeDtypeStruct((peers,) + taper.shape, taper.dtype),
        ),
        in_specs=[hbm] * 3,
        out_specs=(hbm,) * 3,
        scratch_shapes=[dma((3,))] + [dma((peers,))] * 4 + [dma((2, steps, 2))] * 2
        + [dma((2, steps + 1, 2))] * 2,
        compiler_params=pltpu.CompilerParams(collective_id=0, has_side_effects=True),
    )(rows, ids, taper)


def back_kernel(peers, answer, returned, own_sem, send_sems, recv_sems):
    me = lax.axis_index("facet")
    own = pltpu.make_async_copy(answer.at[me], returned.at[me], own_sem)
    own.start()
    greet(peers)
    for copy in swap_blocks(peers, answer, returned, send_sems, recv_sems):
        copy.wait()
    own.wait()


def send_back(peers, answer):
    hbm = pl.BlockSpec(memory_space=pl.ANY)
    dma = pltpu.SemaphoreType.DMA
    return pl.pallas_call(
        functools.partial(back_kernel, peers),
        out_shape=jax.ShapeDtypeStruct(answer.shape, answer.dtype),
        in_specs=[hbm],
        out_specs=hbm,
        scratch_shapes=[dma, dma((peers,)), dma((peers,))],
        compiler_params=pltpu.CompilerParams(collective_id=1, has_side_effects=True),
    )(answer)


def body(visibility, facet_of, cell_of, taper, model):
    peers = lax.axis_size("facet")
    local_rows, columns = visibility.shape
    capacity = 2 * local_rows // peers
    slots = peers * capacity
    cells = model.shape[0]
    gu = gv = math.isqrt(cells)

    target = facet_of[:, 0]
    order = jnp.arange(local_rows, dtype=jnp.int32)
    earlier = (order[:, None] > order[None, :]) & (target[:, None] == target[None, :])
    position = target * capacity + jnp.sum(earlier.astype(jnp.int32), axis=1)
    placed = jnp.arange(slots, dtype=jnp.int32)[:, None] == position[None, :]
    send_rows = jnp.dot(
        placed.astype(jnp.bfloat16), visibility, preferred_element_type=jnp.float32
    ).astype(jnp.bfloat16)
    turned_cell = cell_of % gv * gu + cell_of // gv
    send_cells = jnp.min(jnp.where(placed, turned_cell[None, :], cells), axis=1)

    ids = jnp.pad(send_cells.reshape(peers, 1, capacity), ((0, 0), (0, 0), (0, 128 - capacity)))
    rows, ids, panel = spread(peers, send_rows.reshape(peers, capacity, columns), ids, taper)
    rows = rows.reshape(slots, columns)
    panel = panel.reshape(cells, columns)
    model_next, answer = run_cycle(gu, gv, ids, rows, panel, model)

    returned = send_back(peers, answer.reshape(peers, capacity, columns)).reshape(slots, columns)
    residual = lax.dot_general(
        placed.astype(jnp.bfloat16), returned, (((0,), (0,)), ((), ())),
        preferred_element_type=jnp.float32,
    ).astype(jnp.bfloat16)
    return (model_next, residual)


def solution(mesh):
    both = ("groups", "facet")
    return jax.shard_map(
        body,
        mesh=mesh,
        in_specs=(P(both, None), P(both, None), P(both), P(both, None), P(both, None)),
        out_specs=(P(both, None), P(both, None)),
        check_vma=False,
    )
```

```python
import functools
import math

import jax
import jax.numpy as jnp
from jax import lax
from jax.experimental import pallas as pl
from jax.experimental.pallas import tpu as pltpu
from jax.sharding import PartitionSpec as P

LOOP_GAIN = 0.1
MESH = pl.DeviceIdType.MESH
GROUP = 16
UNROLL = 4
PAD = 8


def dft_table(length, orient):
    ordinal = jnp.arange(length, dtype=jnp.int32)
    phases = ordinal[:, None] * ordinal[None, :] % length
    angles = phases.astype(jnp.float32) * (2.0 * math.pi / length)
    return jnp.concatenate([jnp.cos(angles), orient * jnp.sin(angles)], 1).astype(jnp.bfloat16)


def turned(values):
    half = values.shape[-1] // 2
    lane = lax.broadcasted_iota(jnp.int32, values.shape, 1)
    rolled = pltpu.roll(values, half, 1)
    return jnp.where(lane < half, -rolled, rolled)


def stage(table, slabs):
    columns = slabs[0].shape[1]
    slabs = [slab.astype(jnp.bfloat16) for slab in slabs]
    top = jnp.concatenate(slabs, 1)
    low = jnp.concatenate([turned(slab) for slab in slabs], 1)
    out = jnp.dot(table, jnp.concatenate([top, low], 0), preferred_element_type=jnp.float32)
    return [out[:, k * columns : (k + 1) * columns] for k in range(len(slabs))]


def cycle_kernel(gu, gv, capacity, ids, rows, panel_in, model_in, minus, plus,
                 model_next, answer, wide, cross, picked, panel, model, sems):
    cells = gu * gv
    slots, columns = rows.shape
    half = columns // 2
    runs = capacity // 16
    bits = gu.bit_length() - 1
    assert gu == gv == 1 << bits
    panel_copy = pltpu.make_async_copy(panel_in, panel, sems.at[0])
    model_copy = pltpu.make_async_copy(model_in, model, sems.at[1])
    panel_copy.start()
    model_copy.start()

    def grid_at(i, k):
        return ids[lax.div(i, runs), 0, lax.rem(i, runs) * 16 + k]

    chunk = 512

    @pl.loop(0, cells // chunk)
    def _(i):
        at = pl.ds(pl.multiple_of(i * chunk, chunk), chunk)
        wide[at, :] = jnp.zeros((chunk, columns), jnp.float32)

    panel_copy.wait()

    @pl.loop(0, cells // chunk)
    def _(i):
        at = pl.ds(pl.multiple_of(i * chunk, chunk), chunk)
        cross[at, :] = panel[at, :].astype(jnp.float32)

    wide[pl.ds(cells, 8), :] = jnp.zeros((8, columns), jnp.float32)

    def pick(i, used):
        base = pl.multiple_of(i * 16, 16)
        for k in range(16):
            here = grid_at(i, k)
            used += (here < cells).astype(jnp.int32)
            here = jnp.minimum(here, cells - 1)
            picked[pl.ds(base + k, 1), :] = cross[pl.ds(((here & (gu - 1)) << bits) + (here >> bits), 1), :]
        return used

    used = lax.fori_loop(0, slots // 16, pick, jnp.int32(0))

    lane = lax.broadcasted_iota(jnp.int32, (slots, columns), 1)
    kernel_rows = picked[...]
    swapped = pltpu.roll(kernel_rows, half, 1)
    real = jnp.where(lane < half, kernel_rows, swapped)
    imag = jnp.where(lane < half, swapped, kernel_rows)
    values = rows[...].astype(jnp.float32)
    cross[pl.ds(0, slots), :] = values * real + turned(values) * imag

    @pl.loop(0, slots // 16)
    def _(i):
        base = pl.multiple_of(i * 16, 16)
        for k in range(16):
            at = pl.ds(grid_at(i, k), 1)
            wide[at, :] += cross[pl.ds(base + k, 1), :]

    @pl.loop(0, gv // GROUP, unroll=UNROLL)
    def _(i):
        base = pl.multiple_of(i * (GROUP * gu), GROUP * gu)
        out = stage(minus[...], [wide[pl.ds(base + k * gu, gu), :] for k in range(GROUP)])
        for k in range(GROUP):
            cross[pl.ds(GROUP * i + k, gu, stride=gv + PAD), :] = out[k]

    count = jnp.full((1, columns), used, jnp.int32).astype(jnp.float32)
    gain = LOOP_GAIN / jnp.sqrt(count)
    model_copy.wait()

    @pl.loop(0, gu // GROUP, unroll=UNROLL)
    def _(i):
        base = pl.multiple_of(i * (GROUP * gv), GROUP * gv)
        at = [pl.ds(base + k * gv, gv) for k in range(GROUP)]
        apart = pl.multiple_of(i * (GROUP * (gv + PAD)), 8)
        out = stage(minus[...], [cross[pl.ds(apart + k * (gv + PAD), gv), :] for k in range(GROUP)])
        updated = []
        for k in range(GROUP):
            value = (model[at[k], :].astype(jnp.float32) + gain * out[k]).astype(jnp.bfloat16)
            model[at[k], :] = value
            updated.append(value)
        out = stage(plus[...], updated)
        for k in range(GROUP):
            wide[pl.ds(GROUP * i + k, gv, stride=gu + PAD), :] = out[k]

    next_copy = pltpu.make_async_copy(model, model_next, sems.at[2])
    next_copy.start()

    @pl.loop(0, gv // GROUP, unroll=UNROLL)
    def _(i):
        base = pl.multiple_of(i * (GROUP * gu), GROUP * gu)
        apart = pl.multiple_of(i * (GROUP * (gu + PAD)), 8)
        out = stage(plus[...], [wide[pl.ds(apart + k * (gu + PAD), gu), :] for k in range(GROUP)])
        for k in range(GROUP):
            cross[pl.ds(base + k * gu, gu), :] = out[k]

    cross[pl.ds(cells, 8), :] = jnp.zeros((8, columns), jnp.float32)

    @pl.loop(0, slots // 16)
    def _(i):
        base = pl.multiple_of(i * 16, 16)
        for k in range(16):
            wide[pl.ds(base + k, 1), :] = cross[pl.ds(grid_at(i, k), 1), :]

    kernel_rows = picked[...]
    swapped = pltpu.roll(kernel_rows, half, 1)
    real = jnp.where(lane < half, kernel_rows, swapped)
    imag = jnp.where(lane < half, swapped, kernel_rows)
    found = wide[pl.ds(0, slots), :] * (1.0 / math.sqrt(cells))
    predicted = found * real - turned(found) * imag
    answer[...] = (rows[...].astype(jnp.float32) - predicted).astype(jnp.bfloat16)
    next_copy.wait()


def run_cycle(gu, gv, ids, rows, panel, model):
    cells = gu * gv
    slots, columns = rows.shape
    smem = pl.BlockSpec(memory_space=pltpu.SMEM)
    vmem = pl.BlockSpec(memory_space=pltpu.VMEM)
    hbm = pl.BlockSpec(memory_space=pl.ANY)
    return pl.pallas_call(
        functools.partial(cycle_kernel, gu, gv, slots // ids.shape[0]),
        out_shape=(
            jax.ShapeDtypeStruct((cells, columns), jnp.bfloat16),
            jax.ShapeDtypeStruct((slots, columns), jnp.bfloat16),
        ),
        in_specs=[smem, vmem, hbm, hbm, vmem, vmem],
        out_specs=(hbm, vmem),
        scratch_shapes=[
            pltpu.VMEM((gv * (gu + PAD) + 8, columns), jnp.float32),
            pltpu.VMEM((gu * (gv + PAD) + 8, columns), jnp.float32),
            pltpu.VMEM((slots, columns), jnp.float32),
            pltpu.VMEM((cells, columns), jnp.bfloat16),
            pltpu.VMEM((cells, columns), jnp.bfloat16),
            pltpu.SemaphoreType.DMA((3,)),
        ],
        compiler_params=pltpu.CompilerParams(vmem_limit_bytes=50 * 1024 * 1024),
    )(ids, rows, panel, model, dft_table(gu, -1), dft_table(gu, 1))


def greet(peers):
    me = lax.axis_index("facet")
    barrier = pltpu.get_barrier_semaphore()
    for step in range(1, peers):
        pl.semaphore_signal(
            barrier, inc=1, device_id={"facet": lax.rem(me + step, peers)}, device_id_type=MESH
        )
    pl.semaphore_wait(barrier, peers - 1)


def sent(source, target, send_sem, recv_sem, peer):
    copy = pltpu.make_async_remote_copy(
        src_ref=source, dst_ref=target, send_sem=send_sem, recv_sem=recv_sem,
        device_id={"facet": peer}, device_id_type=MESH,
    )
    copy.start()
    return copy


def swap_blocks(peers, source, target, send_sems, recv_sems):
    me = lax.axis_index("facet")
    copies = []
    for step in range(1, peers):
        peer = lax.rem(me + step, peers)
        copies.append(
            sent(source.at[peer], target.at[me], send_sems.at[step], recv_sems.at[step], peer)
        )
    return copies


def chip_at(place, chips):
    if chips != 8:
        return place
    back = place // 4
    return (1 - back) * (2 * place) + back * (15 - 2 * place)


def place_of(chip, chips):
    if chips != 8:
        return chip
    return chip // 2 + (chip % 2) * (7 - 2 * (chip // 2))


def spread_kernel(peers, rows, ids, taper, rows_out, ids_out, panel, own_sems, row_send, row_recv,
                  id_send, id_recv, ring_send, ring_recv, pass_send, pass_recv):
    me = lax.axis_index("facet")
    chips = peers // 2
    core, place = lax.rem(me, 2), place_of(me // 2, chips)
    sibling = me + 1 - 2 * core
    depth = taper.shape[0]
    half = depth // 2

    def owner(distance):
        return chip_at(lax.rem(place + distance + chips, chips), chips) * 2 + core

    right, left = owner(1), owner(-1)
    greet(peers)

    own = [
        pltpu.make_async_copy(rows.at[me], rows_out.at[me], own_sems.at[0]),
        pltpu.make_async_copy(ids.at[me], ids_out.at[me], own_sems.at[1]),
        pltpu.make_async_copy(taper, panel.at[me], own_sems.at[2]),
    ]

    def goes(way, step, piece):
        return step < chips // 2 - 1 or (step == chips // 2 - 1 and piece == way)

    def ring(way, step, piece):
        part = pl.ds(piece * half, half)
        block = owner(-step if way == 0 else step)
        source = taper.at[part] if step == 0 else panel.at[block, part]
        at = (way, step, piece)
        peer = right if way == 0 else left
        return sent(source, panel.at[block, part], ring_send.at[at], ring_recv.at[at], peer)

    started = {}
    for piece in range(2):
        for way in range(2):
            started[way, 0, piece] = ring(way, 0, piece)
    moves = swap_blocks(peers, ids, ids_out, id_send, id_recv)
    moves += swap_blocks(peers, rows, rows_out, row_send, row_recv)
    passed = [sent(taper, panel.at[me], pass_send.at[0, 0, 0], pass_recv.at[0, 0, 0], sibling)]
    for copy in own:
        copy.start()
    for step in range(chips // 2):
        for piece in range(2):
            for way in range(2):
                if not goes(way, step, piece):
                    continue
                started[way, step, piece].wait_recv()
                if goes(way, step + 1, piece):
                    started[way, step + 1, piece] = ring(way, step + 1, piece)
                block = owner(-(step + 1) if way == 0 else step + 1)
                fresh = panel.at[block, pl.ds(piece * half, half)]
                at = (way, step + 1, piece)
                passed.append(sent(fresh, fresh, pass_send.at[at], pass_recv.at[at], sibling))
    for copy in started.values():
        copy.wait_send()
    for copy in moves + passed:
        copy.wait()
    for copy in own:
        copy.wait()


def spread(peers, rows, ids, taper):
    steps = peers // 4
    hbm = pl.BlockSpec(memory_space=pl.ANY)
    dma = pltpu.SemaphoreType.DMA
    return pl.pallas_call(
        functools.partial(spread_kernel, peers),
        out_shape=(
            jax.ShapeDtypeStruct(rows.shape, rows.dtype),
            jax.ShapeDtypeStruct(ids.shape, ids.dtype),
            jax.ShapeDtypeStruct((peers,) + taper.shape, taper.dtype),
        ),
        in_specs=[hbm] * 3,
        out_specs=(hbm,) * 3,
        scratch_shapes=[dma((3,))] + [dma((peers,))] * 4 + [dma((2, steps, 2))] * 2
        + [dma((2, steps + 1, 2))] * 2,
        compiler_params=pltpu.CompilerParams(collective_id=0, has_side_effects=True),
    )(rows, ids, taper)


def back_kernel(peers, answer, returned, own_sem, send_sems, recv_sems):
    me = lax.axis_index("facet")
    own = pltpu.make_async_copy(answer.at[me], returned.at[me], own_sem)
    own.start()
    greet(peers)
    for copy in swap_blocks(peers, answer, returned, send_sems, recv_sems):
        copy.wait()
    own.wait()


def send_back(peers, answer):
    hbm = pl.BlockSpec(memory_space=pl.ANY)
    dma = pltpu.SemaphoreType.DMA
    return pl.pallas_call(
        functools.partial(back_kernel, peers),
        out_shape=jax.ShapeDtypeStruct(answer.shape, answer.dtype),
        in_specs=[hbm],
        out_specs=hbm,
        scratch_shapes=[dma, dma((peers,)), dma((peers,))],
        compiler_params=pltpu.CompilerParams(collective_id=1, has_side_effects=True),
    )(answer)


def body(visibility, facet_of, cell_of, taper, model):
    peers = lax.axis_size("facet")
    local_rows, columns = visibility.shape
    capacity = 2 * local_rows // peers
    slots = peers * capacity
    cells = model.shape[0]
    gu = gv = math.isqrt(cells)

    target = facet_of[:, 0]
    order = jnp.arange(local_rows, dtype=jnp.int32)
    earlier = (order[:, None] > order[None, :]) & (target[:, None] == target[None, :])
    position = target * capacity + jnp.sum(earlier.astype(jnp.int32), axis=1)
    placed = jnp.arange(slots, dtype=jnp.int32)[:, None] == position[None, :]
    send_rows = jnp.dot(
        placed.astype(jnp.bfloat16), visibility, preferred_element_type=jnp.float32
    ).astype(jnp.bfloat16)
    turned_cell = cell_of % gv * gu + cell_of // gv
    send_cells = jnp.min(jnp.where(placed, turned_cell[None, :], cells), axis=1)

    ids = jnp.pad(send_cells.reshape(peers, 1, capacity), ((0, 0), (0, 0), (0, 128 - capacity)))
    rows, ids, panel = spread(peers, send_rows.reshape(peers, capacity, columns), ids, taper)
    rows = rows.reshape(slots, columns)
    panel = panel.reshape(cells, columns)
    model_next, answer = run_cycle(gu, gv, ids, rows, panel, model)

    returned = send_back(peers, answer.reshape(peers, capacity, columns)).reshape(slots, columns)
    residual = lax.dot_general(
        placed.astype(jnp.bfloat16), returned, (((0,), (0,)), ((), ())),
        preferred_element_type=jnp.float32,
    ).astype(jnp.bfloat16)
    return (model_next, residual)


def solution(mesh):
    both = ("groups", "facet")
    return jax.shard_map(
        body,
        mesh=mesh,
        in_specs=(P(both, None), P(both, None), P(both), P(both, None), P(both, None)),
        out_specs=(P(both, None), P(both, None)),
        check_vma=False,
    )
```

```python
import functools
import math

import jax
import jax.numpy as jnp
from jax import lax
from jax.experimental import pallas as pl
from jax.experimental.pallas import tpu as pltpu
from jax.sharding import PartitionSpec as P

LOOP_GAIN = 0.1
MESH = pl.DeviceIdType.MESH
GROUP = 16
UNROLL = 8
PAD = 8


def dft_table(length, orient):
    ordinal = jnp.arange(length, dtype=jnp.int32)
    phases = ordinal[:, None] * ordinal[None, :] % length
    angles = phases.astype(jnp.float32) * (2.0 * math.pi / length)
    return jnp.concatenate([jnp.cos(angles), orient * jnp.sin(angles)], 1).astype(jnp.bfloat16)


def turned(values):
    half = values.shape[-1] // 2
    lane = lax.broadcasted_iota(jnp.int32, values.shape, 1)
    rolled = pltpu.roll(values, half, 1)
    return jnp.where(lane < half, -rolled, rolled)


def stage(table, slabs):
    columns = slabs[0].shape[1]
    slabs = [slab.astype(jnp.bfloat16) for slab in slabs]
    top = jnp.concatenate(slabs, 1)
    low = jnp.concatenate([turned(slab) for slab in slabs], 1)
    out = jnp.dot(table, jnp.concatenate([top, low], 0), preferred_element_type=jnp.float32)
    return [out[:, k * columns : (k + 1) * columns] for k in range(len(slabs))]


def cycle_kernel(gu, gv, capacity, ids, rows, panel_in, model_in, minus, plus,
                 model_next, answer, wide, cross, picked, panel, model, sems):
    cells = gu * gv
    slots, columns = rows.shape
    half = columns // 2
    runs = capacity // 16
    bits = gu.bit_length() - 1
    assert gu == gv == 1 << bits
    panel_copy = pltpu.make_async_copy(panel_in, panel, sems.at[0])
    model_copy = pltpu.make_async_copy(model_in, model, sems.at[1])
    panel_copy.start()
    model_copy.start()

    def grid_at(i, k):
        return ids[lax.div(i, runs), 0, lax.rem(i, runs) * 16 + k]

    chunk = 512

    @pl.loop(0, cells // chunk)
    def _(i):
        at = pl.ds(pl.multiple_of(i * chunk, chunk), chunk)
        wide[at, :] = jnp.zeros((chunk, columns), jnp.float32)

    panel_copy.wait()

    @pl.loop(0, cells // chunk)
    def _(i):
        at = pl.ds(pl.multiple_of(i * chunk, chunk), chunk)
        cross[at, :] = panel[at, :].astype(jnp.float32)

    wide[pl.ds(cells, 8), :] = jnp.zeros((8, columns), jnp.float32)

    def pick(i, used):
        base = pl.multiple_of(i * 16, 16)
        for k in range(16):
            here = grid_at(i, k)
            used += (here < cells).astype(jnp.int32)
            here = jnp.minimum(here, cells - 1)
            picked[pl.ds(base + k, 1), :] = cross[pl.ds(((here & (gu - 1)) << bits) + (here >> bits), 1), :]
        return used

    used = lax.fori_loop(0, slots // 16, pick, jnp.int32(0))

    lane = lax.broadcasted_iota(jnp.int32, (slots, columns), 1)
    kernel_rows = picked[...]
    swapped = pltpu.roll(kernel_rows, half, 1)
    real = jnp.where(lane < half, kernel_rows, swapped)
    imag = jnp.where(lane < half, swapped, kernel_rows)
    values = rows[...].astype(jnp.float32)
    cross[pl.ds(0, slots), :] = values * real + turned(values) * imag

    @pl.loop(0, slots // 16)
    def _(i):
        base = pl.multiple_of(i * 16, 16)
        for k in range(16):
            at = pl.ds(grid_at(i, k), 1)
            wide[at, :] += cross[pl.ds(base + k, 1), :]

    @pl.loop(0, gv // GROUP, unroll=UNROLL)
    def _(i):
        base = pl.multiple_of(i * (GROUP * gu), GROUP * gu)
        out = stage(minus[...], [wide[pl.ds(base + k * gu, gu), :] for k in range(GROUP)])
        for k in range(GROUP):
            cross[pl.ds(GROUP * i + k, gu, stride=gv + PAD), :] = out[k]

    count = jnp.full((1, columns), used, jnp.int32).astype(jnp.float32)
    gain = LOOP_GAIN / jnp.sqrt(count)
    model_copy.wait()

    @pl.loop(0, gu // GROUP, unroll=UNROLL)
    def _(i):
        base = pl.multiple_of(i * (GROUP * gv), GROUP * gv)
        at = [pl.ds(base + k * gv, gv) for k in range(GROUP)]
        apart = pl.multiple_of(i * (GROUP * (gv + PAD)), 8)
        out = stage(minus[...], [cross[pl.ds(apart + k * (gv + PAD), gv), :] for k in range(GROUP)])
        updated = []
        for k in range(GROUP):
            value = (model[at[k], :].astype(jnp.float32) + gain * out[k]).astype(jnp.bfloat16)
            model[at[k], :] = value
            updated.append(value)
        out = stage(plus[...], updated)
        for k in range(GROUP):
            wide[pl.ds(GROUP * i + k, gv, stride=gu + PAD), :] = out[k]

    next_copy = pltpu.make_async_copy(model, model_next, sems.at[2])
    next_copy.start()

    @pl.loop(0, gv // GROUP, unroll=UNROLL)
    def _(i):
        base = pl.multiple_of(i * (GROUP * gu), GROUP * gu)
        apart = pl.multiple_of(i * (GROUP * (gu + PAD)), 8)
        out = stage(plus[...], [wide[pl.ds(apart + k * (gu + PAD), gu), :] for k in range(GROUP)])
        for k in range(GROUP):
            cross[pl.ds(base + k * gu, gu), :] = out[k]

    cross[pl.ds(cells, 8), :] = jnp.zeros((8, columns), jnp.float32)

    @pl.loop(0, slots // 16)
    def _(i):
        base = pl.multiple_of(i * 16, 16)
        for k in range(16):
            wide[pl.ds(base + k, 1), :] = cross[pl.ds(grid_at(i, k), 1), :]

    kernel_rows = picked[...]
    swapped = pltpu.roll(kernel_rows, half, 1)
    real = jnp.where(lane < half, kernel_rows, swapped)
    imag = jnp.where(lane < half, swapped, kernel_rows)
    found = wide[pl.ds(0, slots), :] * (1.0 / math.sqrt(cells))
    predicted = found * real - turned(found) * imag
    answer[...] = (rows[...].astype(jnp.float32) - predicted).astype(jnp.bfloat16)
    next_copy.wait()


def run_cycle(gu, gv, ids, rows, panel, model):
    cells = gu * gv
    slots, columns = rows.shape
    smem = pl.BlockSpec(memory_space=pltpu.SMEM)
    vmem = pl.BlockSpec(memory_space=pltpu.VMEM)
    hbm = pl.BlockSpec(memory_space=pl.ANY)
    return pl.pallas_call(
        functools.partial(cycle_kernel, gu, gv, slots // ids.shape[0]),
        out_shape=(
            jax.ShapeDtypeStruct((cells, columns), jnp.bfloat16),
            jax.ShapeDtypeStruct((slots, columns), jnp.bfloat16),
        ),
        in_specs=[smem, vmem, hbm, hbm, vmem, vmem],
        out_specs=(hbm, vmem),
        scratch_shapes=[
            pltpu.VMEM((gv * (gu + PAD) + 8, columns), jnp.float32),
            pltpu.VMEM((gu * (gv + PAD) + 8, columns), jnp.float32),
            pltpu.VMEM((slots, columns), jnp.float32),
            pltpu.VMEM((cells, columns), jnp.bfloat16),
            pltpu.VMEM((cells, columns), jnp.bfloat16),
            pltpu.SemaphoreType.DMA((3,)),
        ],
        compiler_params=pltpu.CompilerParams(vmem_limit_bytes=50 * 1024 * 1024),
    )(ids, rows, panel, model, dft_table(gu, -1), dft_table(gu, 1))


def greet(peers):
    me = lax.axis_index("facet")
    barrier = pltpu.get_barrier_semaphore()
    for step in range(1, peers):
        pl.semaphore_signal(
            barrier, inc=1, device_id={"facet": lax.rem(me + step, peers)}, device_id_type=MESH
        )
    pl.semaphore_wait(barrier, peers - 1)


def sent(source, target, send_sem, recv_sem, peer):
    copy = pltpu.make_async_remote_copy(
        src_ref=source, dst_ref=target, send_sem=send_sem, recv_sem=recv_sem,
        device_id={"facet": peer}, device_id_type=MESH,
    )
    copy.start()
    return copy


def swap_blocks(peers, source, target, send_sems, recv_sems):
    me = lax.axis_index("facet")
    copies = []
    for step in range(1, peers):
        peer = lax.rem(me + step, peers)
        copies.append(
            sent(source.at[peer], target.at[me], send_sems.at[step], recv_sems.at[step], peer)
        )
    return copies


def chip_at(place, chips):
    if chips != 8:
        return place
    back = place // 4
    return (1 - back) * (2 * place) + back * (15 - 2 * place)


def place_of(chip, chips):
    if chips != 8:
        return chip
    return chip // 2 + (chip % 2) * (7 - 2 * (chip // 2))


def spread_kernel(peers, rows, ids, taper, rows_out, ids_out, panel, own_sems, row_send, row_recv,
                  id_send, id_recv, ring_send, ring_recv, pass_send, pass_recv):
    me = lax.axis_index("facet")
    chips = peers // 2
    core, place = lax.rem(me, 2), place_of(me // 2, chips)
    sibling = me + 1 - 2 * core
    depth = taper.shape[0]
    half = depth // 2

    def owner(distance):
        return chip_at(lax.rem(place + distance + chips, chips), chips) * 2 + core

    right, left = owner(1), owner(-1)

    own = [
        pltpu.make_async_copy(rows.at[me], rows_out.at[me], own_sems.at[0]),
        pltpu.make_async_copy(ids.at[me], ids_out.at[me], own_sems.at[1]),
        pltpu.make_async_copy(taper, panel.at[me], own_sems.at[2]),
    ]
    for copy in own:
        copy.start()
    greet(peers)

    def goes(way, step, piece):
        return step < chips // 2 - 1 or (step == chips // 2 - 1 and piece == way)

    def ring(way, step, piece):
        part = pl.ds(piece * half, half)
        block = owner(-step if way == 0 else step)
        source = taper.at[part] if step == 0 else panel.at[block, part]
        at = (way, step, piece)
        peer = right if way == 0 else left
        return sent(source, panel.at[block, part], ring_send.at[at], ring_recv.at[at], peer)

    started = {}
    for piece in range(2):
        for way in range(2):
            started[way, 0, piece] = ring(way, 0, piece)
    moves = swap_blocks(peers, ids, ids_out, id_send, id_recv)
    moves += swap_blocks(peers, rows, rows_out, row_send, row_recv)
    passed = [sent(taper, panel.at[me], pass_send.at[0, 0, 0], pass_recv.at[0, 0, 0], sibling)]
    for step in range(chips // 2):
        for piece in range(2):
            for way in range(2):
                if not goes(way, step, piece):
                    continue
                started[way, step, piece].wait_recv()
                if goes(way, step + 1, piece):
                    started[way, step + 1, piece] = ring(way, step + 1, piece)
                block = owner(-(step + 1) if way == 0 else step + 1)
                fresh = panel.at[block, pl.ds(piece * half, half)]
                at = (way, step + 1, piece)
                passed.append(sent(fresh, fresh, pass_send.at[at], pass_recv.at[at], sibling))
    for copy in started.values():
        copy.wait_send()
    for copy in moves + passed:
        copy.wait()
    for copy in own:
        copy.wait()


def spread(peers, rows, ids, taper):
    steps = peers // 4
    hbm = pl.BlockSpec(memory_space=pl.ANY)
    dma = pltpu.SemaphoreType.DMA
    return pl.pallas_call(
        functools.partial(spread_kernel, peers),
        out_shape=(
            jax.ShapeDtypeStruct(rows.shape, rows.dtype),
            jax.ShapeDtypeStruct(ids.shape, ids.dtype),
            jax.ShapeDtypeStruct((peers,) + taper.shape, taper.dtype),
        ),
        in_specs=[hbm] * 3,
        out_specs=(hbm,) * 3,
        scratch_shapes=[dma((3,))] + [dma((peers,))] * 4 + [dma((2, steps, 2))] * 2
        + [dma((2, steps + 1, 2))] * 2,
        compiler_params=pltpu.CompilerParams(collective_id=0, has_side_effects=True),
    )(rows, ids, taper)


def back_kernel(peers, answer, returned, own_sem, send_sems, recv_sems):
    me = lax.axis_index("facet")
    own = pltpu.make_async_copy(answer.at[me], returned.at[me], own_sem)
    own.start()
    greet(peers)
    for copy in swap_blocks(peers, answer, returned, send_sems, recv_sems):
        copy.wait()
    own.wait()


def send_back(peers, answer):
    hbm = pl.BlockSpec(memory_space=pl.ANY)
    dma = pltpu.SemaphoreType.DMA
    return pl.pallas_call(
        functools.partial(back_kernel, peers),
        out_shape=jax.ShapeDtypeStruct(answer.shape, answer.dtype),
        in_specs=[hbm],
        out_specs=hbm,
        scratch_shapes=[dma, dma((peers,)), dma((peers,))],
        compiler_params=pltpu.CompilerParams(collective_id=1, has_side_effects=True),
    )(answer)


def body(visibility, facet_of, cell_of, taper, model):
    peers = lax.axis_size("facet")
    local_rows, columns = visibility.shape
    capacity = 2 * local_rows // peers
    slots = peers * capacity
    cells = model.shape[0]
    gu = gv = math.isqrt(cells)

    target = facet_of[:, 0]
    order = jnp.arange(local_rows, dtype=jnp.int32)
    earlier = (order[:, None] > order[None, :]) & (target[:, None] == target[None, :])
    position = target * capacity + jnp.sum(earlier.astype(jnp.int32), axis=1)
    placed = jnp.arange(slots, dtype=jnp.int32)[:, None] == position[None, :]
    send_rows = jnp.dot(
        placed.astype(jnp.bfloat16), visibility, preferred_element_type=jnp.float32
    ).astype(jnp.bfloat16)
    turned_cell = cell_of % gv * gu + cell_of // gv
    send_cells = jnp.min(jnp.where(placed, turned_cell[None, :], cells), axis=1)

    ids = jnp.pad(send_cells.reshape(peers, 1, capacity), ((0, 0), (0, 0), (0, 128 - capacity)))
    rows, ids, panel = spread(peers, send_rows.reshape(peers, capacity, columns), ids, taper)
    rows = rows.reshape(slots, columns)
    panel = panel.reshape(cells, columns)
    model_next, answer = run_cycle(gu, gv, ids, rows, panel, model)

    returned = send_back(peers, answer.reshape(peers, capacity, columns)).reshape(slots, columns)
    residual = lax.dot_general(
        placed.astype(jnp.bfloat16), returned, (((0,), (0,)), ((), ())),
        preferred_element_type=jnp.float32,
    ).astype(jnp.bfloat16)
    return (model_next, residual)


def solution(mesh):
    both = ("groups", "facet")
    return jax.shard_map(
        body,
        mesh=mesh,
        in_specs=(P(both, None), P(both, None), P(both), P(both, None), P(both, None)),
        out_specs=(P(both, None), P(both, None)),
        check_vma=False,
    )
```
